128 devices in a mesh: leaf: 8 (over x, core), sub: 16 (over z, y).
Axes of the slice: x: 4, y: 4, z: 4, core: 2. Of those that a mesh axis runs over, the one named last changes fastest.
Arguments:
- points: bfloat16 [524288, 128], P(('leaf', 'sub')), may hold values from -5 to 5
- charges: bfloat16 [524288, 64], P(('leaf', 'sub')), may hold values from -0.796875 to 0.796875
- near_leaves: int32 [1024, 12], P(('leaf', 'sub')), may hold values from 0 to 1023, as said below
- leaf_interpolant: bfloat16 [1024, 512, 256], P(('leaf', 'sub')), may hold values from -0.25 to 0.25
- skel_leaf: int32 [1024, 256], P(('leaf', 'sub')), may hold values from 0 to 511, as said below
- interp_mid: bfloat16 [128, 2048, 256], P(('leaf', 'sub')), may hold values from -0.375 to 0.375
- skel_mid: int32 [128, 256], P(('leaf', 'sub')), may hold values from 0 to 2047, as said below
- mid_partners: int32 [128, 4], P(('leaf', 'sub')), may hold values from 0 to 127, as said below
- interp_top: bfloat16 [8, 4096, 256], P('leaf', 'sub'), may hold values from -0.09375 to 0.09375
- skel_top: int32 [8, 256], P('leaf'), may hold values from 0 to 4095, as said below
Outputs:
- potential: float32 [524288, 64], P(('leaf', 'sub'))
The draws below stay inside these ranges and needn't reach their ends.
Inputs may be any that keep to these rules, and one draw needn't show every extreme that they name: `near_leaves`: row l lists leaf l first, then 12 - 1 other different leaves of the same top node. Over the rows of one device's 8 leaves, at most 2 different leaves of any one other device are named. `skel_leaf`: different indices in a row. `skel_mid`: different indices in a row. `skel_top`: different indices in a row. `mid_partners`: different middle nodes of the same top node, never the node itself.
All inputs are finite; a program needn't handle non-finite values.
Results may differ from the reference program's by a relative error of at most 0.008.
Values may be sent and summed in bfloat16 or wider, within the bound.
A program may use at most 128 MiB of HBM per device.

```python
import jax
import jax.numpy as jnp
from jax import lax

LEAF = 512
DIM = 128
RHS = 64
SKEL = 256
NEAR = 12
CAP = 2
FARB = 4
LEAF_DEV = 8
LEAVES = 1024
NPTS = 524288
N_LEAF = 8
N_SUB = 16


def draw_points(key, part):
    base_key = jax.random.fold_in(key, 606)
    rank_key, value_key = jax.random.split(base_key)
    ranks = jax.random.permutation(rank_key, DIM).astype(jnp.float32)
    profile = (ranks + 1.0) ** (-0.625)
    total = jnp.sum(profile * profile)
    scales = profile * jnp.sqrt(5.6 / total)
    values = jax.random.normal(value_key, (NPTS, DIM), jnp.float32)
    return jnp.clip(values * scales[None, :], -5.0, 5.0).astype(jnp.bfloat16)


def draw_near_leaves(key, part):
    devices = N_LEAF * N_SUB
    peer_count = N_SUB // 2
    remote = peer_count * CAP
    total = remote + LEAF_DEV
    base_key = jax.random.fold_in(key, 101)

    def one_device(device):
        device_key = jax.random.fold_in(base_key, device)
        first_key, second_key, third_key = jax.random.split(device_key, 3)
        group = device // N_SUB
        place_in = device % N_SUB
        shifted = jax.random.permutation(first_key, N_SUB - 1)[:peer_count]
        peers = (place_in + 1 + shifted) % N_SUB
        picked = jax.vmap(lambda sub_key: jax.random.permutation(sub_key, LEAF_DEV)[:CAP])(jax.random.split(second_key, peer_count))
        far_ids = ((group * N_SUB + peers)[:, None] * LEAF_DEV + picked).reshape(-1)
        own_ids = device * LEAF_DEV + jnp.arange(LEAF_DEV, dtype=jnp.int32)
        candidates = jnp.concatenate((far_ids, own_ids)).astype(jnp.int32)

        def one_row(member, row_key):
            order = jax.random.permutation(row_key, total).astype(jnp.int32)
            forced = jnp.concatenate((jnp.arange(remote, dtype=jnp.int32) % LEAF_DEV == member, jnp.zeros((LEAF_DEV,), bool))).astype(jnp.int32)
            itself = jnp.concatenate((jnp.zeros((remote,), bool), jnp.arange(LEAF_DEV, dtype=jnp.int32) == member)).astype(jnp.int32)
            scores = order + forced * (4 * total) - itself * (4 * total)
            chosen = jnp.argsort(-scores)[:NEAR - 1]
            return jnp.concatenate((own_ids[member][None], candidates[chosen]))
        return jax.vmap(one_row)(jnp.arange(LEAF_DEV, dtype=jnp.int32), jax.random.split(third_key, LEAF_DEV))
    return jax.vmap(one_device)(jnp.arange(devices, dtype=jnp.int32)).reshape(devices * LEAF_DEV, NEAR).astype(jnp.int32)


def draw_rows(key, salt, count, limit):
    row_random_keys = jax.random.split(jax.random.fold_in(key, salt), count)
    return jax.vmap(lambda row_key: jax.random.permutation(row_key, limit)[:SKEL])(row_random_keys).astype(jnp.int32)


def draw_skel_leaf(key, part):
    return draw_rows(key, 202, LEAF_DEV * N_LEAF * N_SUB, LEAF)


def draw_skel_mid(key, part):
    return draw_rows(key, 303, N_LEAF * N_SUB, LEAF_DEV * SKEL)


def draw_skel_top(key, part):
    return draw_rows(key, 404, N_LEAF, N_SUB * SKEL)


def draw_mid_partners(key, part):
    devices = N_LEAF * N_SUB
    base_key = jax.random.fold_in(key, 505)

    def one_device(device):
        shifted = jax.random.permutation(jax.random.fold_in(base_key, device), N_SUB - 1)[:FARB]
        return device // N_SUB * N_SUB + (device % N_SUB + 1 + shifted) % N_SUB
    return jax.vmap(one_device)(jnp.arange(devices, dtype=jnp.int32)).astype(jnp.int32)


def shard_levels(rng, extent, cuts, smallest, largest):
    level = 1.0
    for axis_at, parts in cuts:
        heights = jax.random.uniform(jax.random.fold_in(jax.random.fold_in(rng, 6), axis_at), (parts,), jnp.float32, smallest / len(cuts), largest / len(cuts))
        level = level * jnp.repeat(jnp.exp(heights), extent[axis_at] // parts).reshape((-1,) + (1,) * (len(extent) - 1 - axis_at))
    return level


def bell_draw(key, extent, scale, bound, cuts=(), kind=jnp.bfloat16):
    factor_of = shard_levels(key, extent, cuts, -0.22, 0.18) if cuts else 1.0
    drawn = jax.random.normal(key, extent, jnp.float32) * scale * factor_of
    return jnp.minimum(jnp.maximum(drawn, -bound), bound).astype(kind)


def setup_inputs(seed: int = 0) -> dict:
    splits = jax.random.split(jax.random.key(seed), 11)
    return {
        "points": draw_points(jax.random.fold_in(splits[10], 71), 0),
        "charges": bell_draw(splits[1], (NPTS, RHS), 0.1, 0.796875, ((0, 128),)),
        "near_leaves": draw_near_leaves(jax.random.fold_in(splits[10], 71), 0),
        "leaf_interpolant": bell_draw(splits[3], (LEAVES, LEAF, SKEL), LEAF ** -0.5, 0.25, ((0, 128),)),
        "skel_leaf": draw_skel_leaf(jax.random.fold_in(splits[10], 71), 0),
        "interp_mid": bell_draw(splits[5], (N_LEAF * N_SUB, LEAF_DEV * SKEL, SKEL), SKEL ** -0.5, 0.375, ((0, 128),)),
        "skel_mid": draw_skel_mid(jax.random.fold_in(splits[10], 71), 0),
        "mid_partners": draw_mid_partners(jax.random.fold_in(splits[10], 71), 0),
        "interp_top": bell_draw(splits[8], (N_LEAF, N_SUB * SKEL, SKEL), (N_SUB * SKEL) ** -0.5, 0.09375, ((0, 8), (1, 16))),
        "skel_top": draw_skel_top(jax.random.fold_in(splits[10], 71), 0),
    }


kernel_rate = 0.25


def kernel_block(target, source):
    products = jnp.einsum("id,kjd->kij", target.astype(jnp.float32), source.astype(jnp.float32))
    target_sq = jnp.sum(jnp.square(target.astype(jnp.float32)), axis=-1)
    source_sq = jnp.sum(jnp.square(source.astype(jnp.float32)), axis=-1)
    distance = target_sq[None, :, None] + source_sq[:, None, :] - 2.0 * products
    return jnp.exp(-kernel_rate * distance).astype(jnp.bfloat16)


def reference(points, charges, near_leaves, leaf_interpolant, skel_leaf, interp_mid, skel_mid, mid_partners, interp_top, skel_top):
    devices = N_LEAF * N_SUB
    leaves = near_leaves.shape[0]
    coords = points.shape[1]
    rhs_count = charges.shape[1]
    leaf_point_coords = points.reshape(leaves, LEAF, coords)
    leaf_source_charges = charges.reshape(leaves, LEAF, rhs_count)

    def near_leaf(leaf_index):
        listed = near_leaves[leaf_index]
        kernel = kernel_block(leaf_point_coords[leaf_index], leaf_point_coords[listed])
        return jnp.einsum("kij,kjr->ir", kernel.astype(jnp.float32), leaf_source_charges[listed].astype(jnp.float32))

    near_sum = lax.map(near_leaf, jnp.arange(leaves, dtype=jnp.int32))
    leaf_upward = jnp.einsum("tmv,tmz->tvz", leaf_interpolant.astype(jnp.float32), leaf_source_charges.astype(jnp.float32)).astype(jnp.bfloat16)
    leaf_skel = jnp.take_along_axis(leaf_point_coords, skel_leaf[:, :, None], axis=1)
    mid_up = jnp.einsum("nqs,nqr->nsr", interp_mid.astype(jnp.float32), leaf_upward.reshape(devices, -1, rhs_count).astype(jnp.float32)).astype(jnp.bfloat16)
    mid_points = jnp.take_along_axis(leaf_skel.reshape(devices, -1, coords), skel_mid[:, :, None], axis=1)

    def mid_node(node):
        listed = mid_partners[node]
        kernel = kernel_block(mid_points[node], mid_points[listed])
        return jnp.einsum("kij,kjr->ir", kernel.astype(jnp.float32), mid_up[listed].astype(jnp.float32))

    mid_sum = lax.map(mid_node, jnp.arange(devices, dtype=jnp.int32))
    top_weight = jnp.einsum("gqs,gqr->gsr", interp_top.astype(jnp.float32), mid_up.reshape(N_LEAF, -1, rhs_count).astype(jnp.float32)).astype(jnp.bfloat16)
    top_points = jnp.take_along_axis(mid_points.reshape(N_LEAF, -1, coords), skel_top[:, :, None], axis=1)

    def top_node(node):
        kernel = kernel_block(top_points[node], top_points)
        keeping = (jnp.arange(N_LEAF, dtype=jnp.int32) != node).astype(jnp.float32)
        return jnp.einsum("kij,kjr,k->ir", kernel.astype(jnp.float32), top_weight.astype(jnp.float32), keeping)

    top_sum = lax.map(top_node, jnp.arange(N_LEAF, dtype=jnp.int32)).astype(jnp.bfloat16)
    spread = jnp.einsum("gqs,gsr->gqr", interp_top.astype(jnp.float32), top_sum.astype(jnp.float32)).reshape(devices, -1, rhs_count)
    mid_total = (mid_sum + spread).astype(jnp.bfloat16)
    leaf_downward = jnp.einsum("nqs,nsr->nqr", interp_mid.astype(jnp.float32), mid_total.astype(jnp.float32)).astype(jnp.bfloat16).reshape(leaves, -1, rhs_count)
    distant_sum = jnp.einsum("xiv,xvq->xiq", leaf_interpolant.astype(jnp.float32), leaf_downward.astype(jnp.float32))
    return (near_sum + distant_sum).reshape(-1, rhs_count)
```

```python
import jax
import jax.numpy as jnp
from jax import lax
from jax.experimental import pallas as pl
from jax.experimental.pallas import tpu as pltpu
from jax.sharding import PartitionSpec as P

F32, BF16, I32 = jnp.float32, jnp.bfloat16, jnp.int32
MESH = pl.DeviceIdType.MESH

RATE = 0.5 * 1.4426950408889634

N_SUB, N_LEAF = 16, 8
LEAVES, LEAF, DIM, RHS, SKEL, NEAR = 8, 512, 128, 64, 256, 12
PACKED = RHS * LEAF // DIM
SLOT = LEAF + PACKED
MID = SKEL + RHS * SKEL // DIM
HALF = MID // 2

GROUPS = ((6, 12), (4, 14), (9, 3), (1, 11), (10,), (5, 15), (7, 13), (2, 8))
WINDOW = 3


def dot(a, b):
    return jnp.dot(a, b, preferred_element_type=F32)


def dot_nt(a, b):
    return lax.dot_general(a, b, (((1,), (1,)), ((), ())), preferred_element_type=F32)


def pieces(x):
    hi = x.astype(BF16).astype(F32)
    mid = (x - hi).astype(BF16).astype(F32)
    return hi, mid, x - hi - mid


def source_side(rows):
    wide = rows.astype(F32)
    square = wide * wide
    high = square.astype(BF16)
    low = (square - high.astype(F32)).astype(BF16)
    half = jnp.full((2 * DIM, DIM), 0.5, BF16)
    hi, mid, lo = pieces(dot(jnp.concatenate((high, low), axis=1), half))
    lane = lax.broadcasted_iota(I32, hi.shape, 1)
    tail = jnp.where(lane < 6, 1.0, 0.0)
    return jnp.where(lane == 0, hi, jnp.where(lane == 1, mid, jnp.where(lane == 2, lo, tail))).astype(BF16)


def target_side(columns):
    wide = columns.astype(F32)
    half = 0.5 * jnp.sum(wide * wide, axis=0, keepdims=True)
    hi, mid, lo = pieces(half)
    row = lax.broadcasted_iota(I32, (16, columns.shape[1]), 0)
    head = jnp.where(row < 3, -1.0, 0.0)
    made = jnp.where(row == 3, -hi, jnp.where(row == 4, -mid, jnp.where(row == 5, -lo, head)))
    return jnp.concatenate((columns, made.astype(BF16), jnp.zeros((DIM - 16, columns.shape[1]), BF16)), axis=0)


def weighted(sources, weights, targets):
    kernel = jnp.exp2(dot(sources, targets) * RATE).astype(BF16)
    return dot(weights, kernel)


def unpacked(block):
    rows = block.shape[0] // RHS
    return jnp.concatenate([block[c * RHS : (c + 1) * RHS] for c in range(rows)], axis=1)


def packed(wide):
    return jnp.concatenate([wide[:, c : c + DIM] for c in range(0, wide.shape[1], DIM)], axis=0)


def exchange_kernel(
    points, charges, near, near_smem, interp_hbm, skel_leaf, mid_hbm, skel_mid, partners, top, skel_top,
    recv, total, targets,
    interp, interp_mid, lists, list_in, charge_pack, send, own_side, skel_cols,
    mid_a, mid_b, scatter, scatter_in, gathered, crossed,
    local_sem, list_s, list_r, near_s, near_r, ma_s, ma_r, mb_s, mb_r, sc_s, sc_r, ga_s, ga_r, cr_s, cr_r,
):
    me, group = lax.axis_index("sub"), lax.axis_index("leaf")
    z, y = me // 4, me % 4
    base = (group * N_SUB + me) * LEAVES

    def peer(k):
        return ((z + k // 4) % 4) * 4 + (y + k % 4) % 4

    def remote(src, dst, s, r, to):
        return pltpu.make_async_remote_copy(
            src_ref=src, dst_ref=dst, send_sem=s, recv_sem=r, device_id=to, device_id_type=MESH
        )

    def in_sub(src, dst, s, r, k):
        return remote(src, dst, s, r, (group, peer(k)))

    load_interp = pltpu.make_async_copy(interp_hbm, interp, local_sem.at[0])
    load_mid = pltpu.make_async_copy(mid_hbm, interp_mid, local_sem.at[1])
    load_interp.start()
    load_mid.start()

    barrier = pltpu.get_barrier_semaphore()
    for k in range(1, N_SUB):
        pl.semaphore_signal(barrier, inc=1, device_id=(group, peer(k)), device_id_type=MESH)
    for j in range(1, N_LEAF):
        pl.semaphore_signal(barrier, inc=1, device_id=((group + j) % N_LEAF, me), device_id_type=MESH)
    lists[...] = jnp.full(lists.shape, -1, I32)
    lists[:, :NEAR] = near[...]
    pl.semaphore_wait(barrier, N_SUB + N_LEAF - 2)

    list_copies = [None] + [
        in_sub(lists, list_in.at[k], list_s.at[k], list_r.at[k], k) for k in range(1, N_SUB)
    ]
    order = [k for ks in GROUPS for k in ks]
    for k in order:
        list_copies[k].start()

    @pl.loop(0, LEAVES)
    def _(l):
        charge_pack[l] = packed(jnp.transpose(charges[l]))

    steps = [(ks, s) for ks in GROUPS for s in range(2)]
    near_copies = []
    chosen = {}

    def advance():
        t = len(near_copies)
        if t >= len(steps):
            return
        if t >= WINDOW:
            for c in near_copies[t - WINDOW]:
                c.wait_send()
        ks, s = steps[t]
        started = []
        for k in ks:
            if s == 0:
                back = (-(k // 4)) % 4 * 4 + (-k) % 4
                list_copies[back].wait_recv()
                here = list_in[back] - base
                inside = (here >= 0) & (here < LEAVES)
                chosen[k] = (
                    jnp.min(jnp.where(inside, here, LEAVES - 1)),
                    jnp.max(jnp.where(inside, here, 0)),
                )
            leaf = chosen[k][s]
            send[k, s, :LEAF, :] = points[leaf]
            send[k, s, LEAF:, :] = charge_pack[leaf]
            c = in_sub(send.at[k, s], recv.at[k, s], near_s.at[k, s], near_r.at[k, s], k)
            c.start()
            started.append(c)
        near_copies.append(started)

    for _ in range(WINDOW):
        advance()

    load_interp.wait()
    load_mid.wait()
    up = jnp.zeros((RHS, SKEL), F32)
    rows_in_leaf = lax.broadcasted_iota(I32, (LEAF, SKEL), 0)

    def upward(l, up):
        columns = jnp.transpose(points[l])
        targets[l] = target_side(columns)
        picks = jnp.where(rows_in_leaf == skel_leaf[pl.ds(l, 1), :], 1.0, 0.0).astype(BF16)
        skel_cols[l] = dot(columns, picks).astype(BF16)
        leaf_up = dot(unpacked(charge_pack[l]), interp[l]).astype(BF16)
        return up + dot(leaf_up, interp_mid[pl.ds(pl.multiple_of(l * SKEL, SKEL), SKEL), :])

    up = lax.fori_loop(0, LEAVES, upward, up)
    mid_up = up.astype(BF16)

    def pick_mid(l, cols):
        row = lax.broadcasted_iota(I32, (SKEL, SKEL), 0) + l * SKEL
        picks = jnp.where(row == skel_mid[...], 1.0, 0.0).astype(BF16)
        return cols + dot(skel_cols[l], picks)

    mid_cols = lax.fori_loop(0, LEAVES, pick_mid, jnp.zeros((DIM, SKEL), F32))
    mid_rows = jnp.transpose(mid_cols).astype(BF16)
    own_mid = jnp.concatenate((mid_rows, packed(mid_up)), axis=0)
    mid_a[0, 0] = own_mid[:HALF]
    mid_b[0, 0] = own_mid[HALF:]
    first = []
    for d in (1, 3, 2):
        first.append((in_sub(mid_a.at[0, 0], mid_a.at[0, d], ma_s.at[0, d], ma_r.at[0, d], d),
                      in_sub(mid_b.at[0, 0], mid_b.at[0, d], mb_s.at[0, d], mb_r.at[0, d], 4 * d)))
        for c in first[-1]:
            c.start()

    row = lax.broadcasted_iota(I32, (SKEL, SKEL), 0) + me * SKEL
    picks = jnp.where(row == skel_top[...], 1.0, 0.0).astype(BF16)
    top_part = jnp.concatenate((dot(mid_up, top[...]), jnp.zeros((DIM - RHS, SKEL), F32)), axis=0)
    scatter[:, :DIM] = jnp.transpose(top_part)
    scatter[:, DIM:] = jnp.transpose(dot(mid_cols.astype(BF16), picks))
    piece = SKEL // N_SUB

    def rows_of(index):
        return pl.ds(pl.multiple_of(index * piece, piece), piece)

    scatter_copies = []
    for k in order:
        c = in_sub(scatter.at[rows_of(peer(k))], scatter_in.at[k], sc_s.at[k], sc_r.at[k], k)
        c.start()
        scatter_copies.append(c)
    advance()

    @pl.loop(0, LEAVES)
    def _(l):
        own_side[l] = source_side(points[l])

    def own_pairs(l):
        result = jnp.zeros((RHS, LEAF), F32)
        for part in range(0, LEAVES, 4):
            rows, weights = [], []
            for m in range(part, part + 4):
                named = near_smem[l, 0] == base + m
                for e in range(1, NEAR):
                    named = named | (near_smem[l, e] == base + m)
                flag = jnp.where(named, 1.0, 0.0)
                rows.append(jnp.concatenate((points[m], own_side[m]), axis=1))
                weights.append((unpacked(charge_pack[m]).astype(F32) * flag).astype(BF16))
            result += weighted(jnp.concatenate(rows, axis=0), jnp.concatenate(weights, axis=1), targets[l])
        total[l] = result

    def own_chunk(begin, end):
        pl.loop(begin, end)(own_pairs)

    own_chunk(0, 2)
    advance()

    for pair in first:
        for c in pair:
            c.wait_recv()
    second = []
    for d in (1, 3, 2):
        second.append((in_sub(mid_a.at[0], mid_a.at[d], ma_s.at[1, d], ma_r.at[1, d], 4 * d),
                       in_sub(mid_b.at[0], mid_b.at[d], mb_s.at[1, d], mb_r.at[1, d], d)))
        for c in second[-1]:
            c.start()
    advance()

    for c in scatter_copies:
        c.wait_recv()
    summed = scatter[rows_of(me), :]
    for k in range(1, N_SUB):
        summed = summed + scatter_in[k]
    gathered[rows_of(me), :] = summed.astype(BF16)
    gather_copies = []
    for k in order:
        c = in_sub(gathered.at[rows_of(me)], gathered.at[rows_of(me)], ga_s.at[k], ga_r.at[k], k)
        c.start()
        gather_copies.append(c)

    own_chunk(2, 4)
    advance()
    own_chunk(4, 6)
    advance()

    for c in gather_copies:
        c.wait_recv()
    cross_copies = []
    for j in (1, 7, 2, 6, 3, 5, 4):
        c = remote(gathered, crossed.at[j - 1], cr_s.at[j - 1], cr_r.at[j - 1], ((group + j) % N_LEAF, me))
        c.start()
        cross_copies.append(c)
    own_chunk(6, 8)
    advance()
    advance()

    for pair in second:
        for c in pair:
            c.wait_recv()
    mid_targets = target_side(mid_cols.astype(BF16))
    rows, weights = [], []
    for p in range(4):
        node = partners[0, p] - group * N_SUB
        dz, dy = (z + 4 - node // 4) % 4, (y + 4 - node % 4) % 4
        block = jnp.concatenate((mid_a[dz, dy], mid_b[dy, dz]), axis=0)
        rows.append(jnp.concatenate((block[:SKEL], source_side(block[:SKEL])), axis=1))
        weights.append(unpacked(block[SKEL:]))
    mid_sum = weighted(jnp.concatenate(rows, axis=0), jnp.concatenate(weights, axis=1), mid_targets)
    advance()

    for c in cross_copies:
        c.wait_recv()
    top_targets = target_side(jnp.transpose(gathered[:, DIM:].astype(F32)).astype(BF16))

    def top_from(j, acc):
        rows = crossed[j, :, DIM:]
        weights = jnp.transpose(crossed[j, :, :DIM].astype(F32)).astype(BF16)[:RHS]
        return acc + weighted(jnp.concatenate((rows, source_side(rows)), axis=1), weights, top_targets)

    top_sum = lax.fori_loop(0, N_LEAF - 1, top_from, jnp.zeros((RHS, SKEL), F32)).astype(BF16)
    mid_total = (mid_sum + dot_nt(top_sum, top[...])).astype(BF16)
    advance()

    @pl.loop(0, LEAVES)
    def _(l):
        down = dot_nt(mid_total, interp_mid[pl.ds(pl.multiple_of(l * SKEL, SKEL), SKEL), :]).astype(BF16)
        total[l] += dot_nt(down, interp[l])

    while len(near_copies) < len(steps):
        advance()
    for t, copies in enumerate(near_copies):
        for c in copies:
            if t >= len(steps) - WINDOW:
                c.wait_send()
            c.wait_recv()
    for c in list_copies[1:] + scatter_copies + gather_copies + cross_copies:
        c.wait_send()
    for pair in first + second:
        for c in pair:
            c.wait_send()


def near_kernel(near, recv, targets, total, out, side, listed, count, lowest, used):
    me, group = lax.axis_index("sub"), lax.axis_index("leaf")
    z, y = me // 4, me % 4
    base = group * N_SUB * LEAVES

    for i in range(N_SUB):
        lowest[i] = LEAVES
    for i in range(2 * N_SUB):
        used[i] = 0

    @pl.loop(0, LEAVES)
    def _(l):
        for e in range(1, NEAR):
            named = near[l, e] - base
            owner, leaf = named // LEAVES, named % LEAVES
            lowest[owner] = jnp.minimum(lowest[owner], leaf)

    @pl.loop(0, LEAVES)
    def _(l):
        held = jnp.int32(0)
        for e in range(1, NEAR):
            named = near[l, e] - base
            owner, leaf = named // LEAVES, named % LEAVES
            shift = ((z + 4 - owner // 4) % 4) * 4 + (y + 4 - owner % 4) % 4
            slot = 2 * shift + jnp.where(leaf == lowest[owner], 0, 1)
            listed[l, held] = slot
            there = jnp.where(owner == me, 0, 1)
            used[slot] = jnp.maximum(used[slot], there)
            held = held + there
        count[l] = held

    @pl.loop(2, 2 * N_SUB)
    def _(i):
        @pl.when(used[i] > 0)
        def _():
            side[i] = source_side(recv[i, :LEAF, :])

    @pl.loop(0, LEAVES)
    def _(l):
        held = count[l]

        def four(n, acc):
            rows, weights = [], []
            for u in range(4):
                e = n * 4 + u
                real = e < held
                slot = listed[l, jnp.where(real, e, 0)]
                rows.append(jnp.concatenate((recv[slot, :LEAF, :], side[slot]), axis=1))
                flag = jnp.where(real, 1.0, 0.0)
                weights.append((unpacked(recv[slot, LEAF:, :]).astype(F32) * flag).astype(BF16))
            return acc + weighted(jnp.concatenate(rows, axis=0), jnp.concatenate(weights, axis=1), targets[l])

        acc = lax.fori_loop(0, (held + 3) // 4, four, total[l])
        out[l] = jnp.transpose(acc)


def body(
    points, charges, near_leaves, leaf_interpolant, skel_leaf,
    interp_mid, skel_mid, mid_partners, interp_top, skel_top,
):
    vmem, smem, hbm = (pl.BlockSpec(memory_space=m) for m in (pltpu.VMEM, pltpu.SMEM, pl.ANY))
    dma = pltpu.SemaphoreType.DMA
    recv, total, targets = pl.pallas_call(
        exchange_kernel,
        out_shape=(
            jax.ShapeDtypeStruct((N_SUB, 2, SLOT, DIM), BF16),
            jax.ShapeDtypeStruct((LEAVES, RHS, LEAF), F32),
            jax.ShapeDtypeStruct((LEAVES, 2 * DIM, LEAF), BF16),
        ),
        in_specs=[vmem, vmem, vmem, smem, hbm, vmem, hbm, vmem, smem, vmem, vmem],
        out_specs=(hbm, vmem, vmem),
        scratch_shapes=[
            pltpu.VMEM((LEAVES, LEAF, SKEL), BF16),
            pltpu.VMEM((LEAVES * SKEL, SKEL), BF16),
            pltpu.VMEM((LEAVES, DIM), I32),
            pltpu.VMEM((N_SUB, LEAVES, DIM), I32),
            pltpu.VMEM((LEAVES, PACKED, DIM), BF16),
            pltpu.VMEM((N_SUB, 2, SLOT, DIM), BF16),
            pltpu.VMEM((LEAVES, LEAF, DIM), BF16),
            pltpu.VMEM((LEAVES, DIM, SKEL), BF16),
            pltpu.VMEM((4, 4, HALF, DIM), BF16),
            pltpu.VMEM((4, 4, HALF, DIM), BF16),
            pltpu.VMEM((SKEL, 2 * DIM), F32),
            pltpu.VMEM((N_SUB, SKEL // N_SUB, 2 * DIM), F32),
            pltpu.VMEM((SKEL, 2 * DIM), BF16),
            pltpu.VMEM((N_LEAF - 1, SKEL, 2 * DIM), BF16),
            dma((2,)),
            dma((N_SUB,)), dma((N_SUB,)),
            dma((N_SUB, 2)), dma((N_SUB, 2)),
            dma((2, 4)), dma((2, 4)), dma((2, 4)), dma((2, 4)),
            dma((N_SUB,)), dma((N_SUB,)),
            dma((N_SUB,)), dma((N_SUB,)),
            dma((N_LEAF - 1,)), dma((N_LEAF - 1,)),
        ],
        compiler_params=pltpu.CompilerParams(
            collective_id=0, has_side_effects=True, vmem_limit_bytes=56 << 20
        ),
    )(
        points.reshape(LEAVES, LEAF, DIM), charges.reshape(LEAVES, LEAF, RHS), near_leaves, near_leaves,
        leaf_interpolant, skel_leaf, interp_mid[0], skel_mid, mid_partners, interp_top[0], skel_top,
    )
    out = pl.pallas_call(
        near_kernel,
        out_shape=jax.ShapeDtypeStruct((LEAVES, LEAF, RHS), F32),
        in_specs=[smem, vmem, vmem, vmem],
        out_specs=vmem,
        scratch_shapes=[
            pltpu.VMEM((2 * N_SUB, LEAF, DIM), BF16),
            pltpu.SMEM((LEAVES, 16), I32),
            pltpu.SMEM((LEAVES,), I32),
            pltpu.SMEM((N_SUB,), I32),
            pltpu.SMEM((2 * N_SUB,), I32),
        ],
        compiler_params=pltpu.CompilerParams(vmem_limit_bytes=56 << 20),
    )(near_leaves, recv.reshape(2 * N_SUB, SLOT, DIM), targets, total)
    return out.reshape(LEAVES * LEAF, RHS)


def solution(mesh):
    placed = (
        P(("leaf", "sub"), None),
        P(("leaf", "sub"), None),
        P(("leaf", "sub"), None),
        P(("leaf", "sub"), None, None),
        P(("leaf", "sub"), None),
        P(("leaf", "sub"), None, None),
        P(("leaf", "sub"), None),
        P(("leaf", "sub"), None),
        P("leaf", "sub", None),
        P("leaf", None),
    )
    return jax.shard_map(
        body, mesh=mesh, in_specs=placed, out_specs=P(("leaf", "sub"), None), check_vma=False
    )
```

```python
import jax
import jax.numpy as jnp
from jax import lax
from jax.experimental import pallas as pl
from jax.experimental.pallas import tpu as pltpu
from jax.sharding import PartitionSpec as P

F32, BF16, I32 = jnp.float32, jnp.bfloat16, jnp.int32
MESH = pl.DeviceIdType.MESH

RATE = 0.5 * 1.4426950408889634

N_SUB, N_LEAF = 16, 8
LEAVES, LEAF, DIM, RHS, SKEL, NEAR = 8, 512, 128, 64, 256, 12
PACKED = RHS * LEAF // DIM
SLOT = LEAF + PACKED
MID = SKEL + RHS * SKEL // DIM
HALF = MID // 2

GROUPS = ((6, 12), (4, 14), (9, 3), (1, 11), (10,), (5, 15), (7, 13), (2, 8))
WINDOW = 5
ORDER = [k for ks in GROUPS for k in ks]
EARLY, MIDDLE = 8, 11
STAGE = 64


def dot(a, b):
    return jnp.dot(a, b, preferred_element_type=F32)


def dot_nt(a, b):
    return lax.dot_general(a, b, (((1,), (1,)), ((), ())), preferred_element_type=F32)


def pieces(x):
    hi = x.astype(BF16).astype(F32)
    mid = (x - hi).astype(BF16).astype(F32)
    return hi, mid, x - hi - mid


def source_side(rows):
    wide = rows.astype(F32)
    square = wide * wide
    high = square.astype(BF16)
    low = (square - high.astype(F32)).astype(BF16)
    half = jnp.full((2 * DIM, DIM), 0.5, BF16)
    hi, mid, lo = pieces(dot(jnp.concatenate((high, low), axis=1), half))
    lane = lax.broadcasted_iota(I32, hi.shape, 1)
    tail = jnp.where(lane < 6, 1.0, 0.0)
    return jnp.where(lane == 0, hi, jnp.where(lane == 1, mid, jnp.where(lane == 2, lo, tail))).astype(BF16)


def target_side(columns):
    wide = columns.astype(F32)
    half = 0.5 * jnp.sum(wide * wide, axis=0, keepdims=True)
    hi, mid, lo = pieces(half)
    row = lax.broadcasted_iota(I32, (16, columns.shape[1]), 0)
    head = jnp.where(row < 3, -1.0, 0.0)
    made = jnp.where(row == 3, -hi, jnp.where(row == 4, -mid, jnp.where(row == 5, -lo, head)))
    return jnp.concatenate((columns, made.astype(BF16), jnp.zeros((DIM - 16, columns.shape[1]), BF16)), axis=0)


def weighted(sources, weights, targets):
    kernel = jnp.exp2(dot(sources, targets) * RATE).astype(BF16)
    return dot(weights, kernel)


def unpacked(block):
    rows = block.shape[0] // RHS
    return jnp.concatenate([block[c * RHS : (c + 1) * RHS] for c in range(rows)], axis=1)


def packed(wide):
    return jnp.concatenate([wide[:, c : c + DIM] for c in range(0, wide.shape[1], DIM)], axis=0)


def sorted_lists(lists, first_leaf, z, y):
    shape = (128, 128)
    sub, lane = lax.broadcasted_iota(I32, shape, 0), lax.broadcasted_iota(I32, shape, 1)

    def down(row):
        return jnp.transpose(jnp.broadcast_to(row.astype(F32), shape)).astype(I32)

    tall = jnp.concatenate([jnp.broadcast_to(lists[l : l + 1, :], (16, 128)) for l in range(LEAVES)], axis=0)
    mine = jnp.where((sub % 16 == lane) & (sub % 16 < NEAR), tall - first_leaf, 0)
    column = jnp.broadcast_to(jnp.sum(mine.astype(F32), axis=1, keepdims=True), shape)
    va, vb = column.astype(I32), jnp.transpose(column).astype(I32)
    before = (sub % 16 < NEAR) & (va // LEAVES == vb // LEAVES) & (va < vb)
    slot = jnp.max(jnp.where(before, 1.0, 0.0), axis=0, keepdims=True).astype(I32)
    owner, place = vb[:1] // LEAVES, lane[:1] % 16
    shift = (z + 4 - owner // 4) % 4 * 4 + (y + 4 - owner % 4) % 4
    turn = jnp.zeros_like(shift)
    for at, k in enumerate(ORDER):
        turn = jnp.where(shift == k, at, turn)
    stage = jnp.where(turn < EARLY, 0, jnp.where(turn < MIDDLE, 1, 2))
    stage = jnp.where(place < NEAR, jnp.where(shift == 0, 3, stage), 4)
    key, code = stage * 16 + place, stage * STAGE + 2 * turn + slot
    same = sub // 16 == lane // 16
    rank = jnp.sum(jnp.where(same & (down(key) < key), 1.0, 0.0), axis=0, keepdims=True).astype(I32)
    chosen = jnp.where(same & (down(rank) == lane % 16), down(code), 0)
    return jnp.sum(chosen.astype(F32), axis=0, keepdims=True).astype(I32)


def progress(codes, l):
    first = both = remote = jnp.int32(0)
    for e in range(NEAR):
        code = codes[0, l * 16 + e]
        first += jnp.where(code < STAGE, 1, 0)
        both += jnp.where(code < 2 * STAGE, 1, 0)
        remote += jnp.where(code < 3 * STAGE, 1, 0)
    first = jnp.minimum(first, 4)
    return first, first + jnp.minimum(both - first, 4), remote


def listed_pairs(codes, l, start, limit, held, side, target):
    rows, weights = [], []
    spare = jnp.where(codes[0, l * 16 + start] < limit, codes[0, l * 16 + start], 0)
    for u in range(4):
        code = codes[0, l * 16 + start + u]
        real = code < limit
        slot = jnp.clip(jnp.where(real, code, spare) % STAGE, 0, held.shape[0] - 1)
        rows.append(jnp.concatenate((held[slot, :LEAF, :], side[slot]), axis=1))
        flag = jnp.where(real, 1.0, 0.0)
        weights.append((unpacked(held[slot, LEAF:, :]).astype(F32) * flag).astype(BF16))
    return weighted(jnp.concatenate(rows, axis=0), jnp.concatenate(weights, axis=1), target)


def exchange_kernel(
    points, charges, near, near_smem, interp_hbm, skel_leaf, mid_hbm, skel_mid, partners, top, skel_top,
    recv, total, targets, codes_out,
    interp, interp_mid, lists, list_in, charge_pack, send, own_side, skel_cols,
    mid_a, mid_b, scatter, scatter_in, gathered, crossed, early, held, side, codes,
    local_sem, list_s, list_r, near_s, near_r, ma_s, ma_r, mb_s, mb_r, sc_s, sc_r, ga_s, ga_r, cr_s, cr_r,
):
    me, group = lax.axis_index("sub"), lax.axis_index("leaf")
    z, y = me // 4, me % 4
    base = (group * N_SUB + me) * LEAVES

    def peer(k):
        return ((z + k // 4) % 4) * 4 + (y + k % 4) % 4

    def remote(src, dst, s, r, to):
        return pltpu.make_async_remote_copy(
            src_ref=src, dst_ref=dst, send_sem=s, recv_sem=r, device_id=to, device_id_type=MESH
        )

    def in_sub(src, dst, s, r, k):
        return remote(src, dst, s, r, (group, peer(k)))

    load_interp = pltpu.make_async_copy(interp_hbm, interp, local_sem.at[0])
    load_mid = pltpu.make_async_copy(mid_hbm, interp_mid, local_sem.at[1])
    load_interp.start()
    load_mid.start()

    barrier = pltpu.get_barrier_semaphore()
    for k in range(1, N_SUB):
        pl.semaphore_signal(barrier, inc=1, device_id=(group, peer(k)), device_id_type=MESH)
    for j in range(1, N_LEAF):
        pl.semaphore_signal(barrier, inc=1, device_id=((group + j) % N_LEAF, me), device_id_type=MESH)
    lists[...] = jnp.full(lists.shape, -1, I32)
    lists[:, :NEAR] = near[...]
    pl.semaphore_wait(barrier, N_SUB + N_LEAF - 2)

    list_copies = [None] + [
        in_sub(lists, list_in.at[k], list_s.at[k], list_r.at[k], k) for k in range(1, N_SUB)
    ]
    order = ORDER
    for k in order:
        list_copies[k].start()

    @pl.loop(0, LEAVES)
    def _(l):
        charge_pack[l] = packed(charges[:, pl.ds(pl.multiple_of(l * LEAF, LEAF), LEAF)])

    steps = [(ks, s) for ks in GROUPS for s in range(2)]
    near_copies = []
    chosen = {}

    def advance():
        t = len(near_copies)
        if t >= len(steps):
            return
        if t >= WINDOW:
            for c in near_copies[t - WINDOW]:
                c.wait_send()
        ks, s = steps[t]
        started = []
        for k in ks:
            if s == 0:
                back = (-(k // 4)) % 4 * 4 + (-k) % 4
                list_copies[back].wait_recv()
                here = list_in[back] - base
                inside = (here >= 0) & (here < LEAVES)
                chosen[k] = (
                    jnp.min(jnp.where(inside, here, LEAVES - 1)),
                    jnp.max(jnp.where(inside, here, 0)),
                )
            leaf = chosen[k][s]
            send[k, s, :LEAF, :] = points[leaf]
            send[k, s, LEAF:, :] = charge_pack[leaf]
            at = 2 * ORDER.index(k) + s
            if at < 2 * EARLY:
                landing = early.at[at]
            elif at < 2 * MIDDLE:
                landing = held.at[at]
            else:
                landing = recv.at[at]
            c = in_sub(send.at[k, s], landing, near_s.at[k, s], near_r.at[k, s], k)
            c.start()
            started.append(c)
        near_copies.append(started)

    for _ in range(WINDOW):
        advance()

    codes_out[...] = jnp.broadcast_to(sorted_lists(lists, group * N_SUB * LEAVES, z, y), codes_out.shape)
    save_codes = pltpu.make_async_copy(codes_out, codes, local_sem.at[2])
    save_codes.start()

    load_interp.wait()
    load_mid.wait()
    up = jnp.zeros((RHS, SKEL), F32)
    rows_in_leaf = lax.broadcasted_iota(I32, (LEAF, SKEL), 0)

    def upward(l, up):
        columns = jnp.transpose(points[l])
        targets[l] = target_side(columns)
        picks = jnp.where(rows_in_leaf == skel_leaf[pl.ds(l, 1), :], 1.0, 0.0).astype(BF16)
        skel_cols[l] = dot(columns, picks).astype(BF16)
        leaf_up = dot(unpacked(charge_pack[l]), interp[l]).astype(BF16)
        return up + dot(leaf_up, interp_mid[pl.ds(pl.multiple_of(l * SKEL, SKEL), SKEL), :])

    up = lax.fori_loop(0, LEAVES, upward, up)
    mid_up = up.astype(BF16)

    def pick_mid(l, cols):
        row = lax.broadcasted_iota(I32, (SKEL, SKEL), 0) + l * SKEL
        picks = jnp.where(row == skel_mid[...], 1.0, 0.0).astype(BF16)
        return cols + dot(skel_cols[l], picks)

    mid_cols = lax.fori_loop(0, LEAVES, pick_mid, jnp.zeros((DIM, SKEL), F32))
    mid_rows = jnp.transpose(mid_cols).astype(BF16)
    own_mid = jnp.concatenate((mid_rows, packed(mid_up)), axis=0)
    mid_a[0, 0] = own_mid[:HALF]
    mid_b[0, 0] = own_mid[HALF:]
    first = []
    for d in (1, 3, 2):
        first.append((in_sub(mid_a.at[0, 0], mid_a.at[0, d], ma_s.at[0, d], ma_r.at[0, d], d),
                      in_sub(mid_b.at[0, 0], mid_b.at[0, d], mb_s.at[0, d], mb_r.at[0, d], 4 * d)))
        for c in first[-1]:
            c.start()

    row = lax.broadcasted_iota(I32, (SKEL, SKEL), 0) + me * SKEL
    picks = jnp.where(row == skel_top[...], 1.0, 0.0).astype(BF16)
    top_part = jnp.concatenate((dot(mid_up, top[...]), jnp.zeros((DIM - RHS, SKEL), F32)), axis=0)
    scatter[:, :DIM] = jnp.transpose(top_part)
    scatter[:, DIM:] = jnp.transpose(dot(mid_cols.astype(BF16), picks))
    piece = SKEL // N_SUB

    def rows_of(index):
        return pl.ds(pl.multiple_of(index * piece, piece), piece)

    scatter_copies = []
    for k in order:
        c = in_sub(scatter.at[rows_of(peer(k))], scatter_in.at[k], sc_s.at[k], sc_r.at[k], k)
        c.start()
        scatter_copies.append(c)
    advance()

    @pl.loop(0, LEAVES)
    def _(l):
        own_side[l] = source_side(points[l])

    def own_pairs(l):
        result = jnp.zeros((RHS, LEAF), F32)
        for part in range(0, LEAVES, 4):
            rows, weights = [], []
            for m in range(part, part + 4):
                named = near_smem[l, 0] == base + m
                for e in range(1, NEAR):
                    named = named | (near_smem[l, e] == base + m)
                flag = jnp.where(named, 1.0, 0.0)
                rows.append(jnp.concatenate((points[m], own_side[m]), axis=1))
                weights.append((unpacked(charge_pack[m]).astype(F32) * flag).astype(BF16))
            result += weighted(jnp.concatenate(rows, axis=0), jnp.concatenate(weights, axis=1), targets[l])
        total[l] = result

    def own_chunk(begin, end):
        pl.loop(begin, end)(own_pairs)

    own_chunk(0, 2)
    advance()
    own_chunk(2, 4)
    advance()

    for pair in first:
        for c in pair:
            c.wait_recv()
    second = []
    for d in (1, 3, 2):
        second.append((in_sub(mid_a.at[0], mid_a.at[d], ma_s.at[1, d], ma_r.at[1, d], 4 * d),
                       in_sub(mid_b.at[0], mid_b.at[d], mb_s.at[1, d], mb_r.at[1, d], d)))
        for c in second[-1]:
            c.start()

    for c in scatter_copies:
        c.wait_recv()
    summed = scatter[rows_of(me), :]
    for k in range(1, N_SUB):
        summed = summed + scatter_in[k]
    gathered[rows_of(me), :] = summed.astype(BF16)
    gather_copies = []
    for k in order:
        c = in_sub(gathered.at[rows_of(me)], gathered.at[rows_of(me)], ga_s.at[k], ga_r.at[k], k)
        c.start()
        gather_copies.append(c)

    advance()
    own_chunk(4, 6)
    advance()
    own_chunk(6, 8)
    advance()

    save_codes.wait()

    def arrived(begin, end):
        for ks, copies in zip([g for g in GROUPS for _ in range(2)], near_copies):
            for k, c in zip(ks, copies):
                if begin <= ORDER.index(k) < end:
                    c.wait_recv()

    arrived(0, EARLY)
    keep_early = pltpu.make_async_copy(early, held.at[pl.ds(0, 2 * EARLY)], local_sem.at[3])
    keep_early.start()

    @pl.loop(0, 2 * EARLY)
    def _(i):
        side[i] = source_side(early[i, :LEAF, :])

    advance()

    def first_pass(l):
        total[l] += listed_pairs(codes, l, 0, STAGE, early, side, targets[l])

    for begin in range(0, LEAVES, 2):
        pl.loop(begin, begin + 2)(first_pass)
        advance()
        if begin == 2:
            for c in gather_copies:
                c.wait_recv()
            cross_copies = []
            for j in (1, 7, 2, 6, 3, 5, 4):
                c = remote(gathered, crossed.at[j - 1], cr_s.at[j - 1], cr_r.at[j - 1], ((group + j) % N_LEAF, me))
                c.start()
                cross_copies.append(c)
    while len(near_copies) < len(steps):
        advance()

    for pair in second:
        for c in pair:
            c.wait_recv()
    mid_targets = target_side(mid_cols.astype(BF16))
    rows, weights = [], []
    for p in range(4):
        node = partners[0, p] - group * N_SUB
        dz, dy = (z + 4 - node // 4) % 4, (y + 4 - node % 4) % 4
        block = jnp.concatenate((mid_a[dz, dy], mid_b[dy, dz]), axis=0)
        rows.append(jnp.concatenate((block[:SKEL], source_side(block[:SKEL])), axis=1))
        weights.append(unpacked(block[SKEL:]))
    mid_sum = weighted(jnp.concatenate(rows, axis=0), jnp.concatenate(weights, axis=1), mid_targets)

    keep_early.wait()
    arrived(EARLY, MIDDLE)
    keep_held = pltpu.make_async_copy(held, recv.at[pl.ds(0, 2 * MIDDLE)], local_sem.at[4])
    keep_held.start()

    @pl.loop(2 * EARLY, 2 * MIDDLE)
    def _(i):
        side[i] = source_side(held[i, :LEAF, :])

    @pl.loop(0, LEAVES)
    def _(l):
        start, _, _ = progress(codes, l)
        total[l] += listed_pairs(codes, l, start, 2 * STAGE, held, side, targets[l])

    for c in cross_copies:
        c.wait_recv()
    top_targets = target_side(jnp.transpose(gathered[:, DIM:].astype(F32)).astype(BF16))

    def top_from(j, acc):
        rows = crossed[j, :, DIM:]
        weights = jnp.transpose(crossed[j, :, :DIM].astype(F32)).astype(BF16)[:RHS]
        return acc + weighted(jnp.concatenate((rows, source_side(rows)), axis=1), weights, top_targets)

    top_sum = lax.fori_loop(0, N_LEAF - 1, top_from, jnp.zeros((RHS, SKEL), F32)).astype(BF16)
    mid_total = (mid_sum + dot_nt(top_sum, top[...])).astype(BF16)

    @pl.loop(0, LEAVES)
    def _(l):
        down = dot_nt(mid_total, interp_mid[pl.ds(pl.multiple_of(l * SKEL, SKEL), SKEL), :]).astype(BF16)
        total[l] += dot_nt(down, interp[l])

    for t, copies in enumerate(near_copies):
        for c in copies:
            if t >= len(steps) - WINDOW:
                c.wait_send()
    for c in list_copies[1:] + scatter_copies + gather_copies + cross_copies:
        c.wait_send()
    for pair in first + second:
        for c in pair:
            c.wait_send()
    keep_held.wait()
    arrived(MIDDLE, N_SUB)


def near_kernel(codes, recv, targets, total, out, held, side, used, sem):
    slots = held.shape[0]
    for i in range(STAGE):
        used[i] = 0

    @pl.loop(0, LEAVES)
    def _(l):
        _, begin, end = progress(codes, l)
        for e in range(NEAR):
            slot = codes[0, l * 16 + e] % STAGE
            used[slot] = jnp.maximum(used[slot], jnp.where((begin <= e) & (e < end), 1, 0))

    def copy(i):
        return pltpu.make_async_copy(recv.at[i], held.at[i], sem.at[i])

    @pl.loop(0, slots)
    def _(i):
        pl.when(used[i] > 0)(lambda: copy(i).start())

    @pl.loop(0, slots)
    def _(i):
        @pl.when(used[i] > 0)
        def _():
            copy(i).wait()
            side[i] = source_side(held[i, :LEAF, :])

    @pl.loop(0, LEAVES)
    def _(l):
        _, begin, end = progress(codes, l)

        def four(n, acc):
            return acc + listed_pairs(codes, l, begin + 4 * n, 3 * STAGE, held, side, targets[l])

        acc = lax.fori_loop(0, (end - begin + 3) // 4, four, total[l])
        out[:, pl.ds(pl.multiple_of(l * LEAF, LEAF), LEAF)] = acc


def body(
    points, charges, near_leaves, leaf_interpolant, skel_leaf,
    interp_mid, skel_mid, mid_partners, interp_top, skel_top,
):
    vmem, smem, hbm = (pl.BlockSpec(memory_space=m) for m in (pltpu.VMEM, pltpu.SMEM, pl.ANY))
    dma = pltpu.SemaphoreType.DMA
    slots = 2 * (N_SUB - 1)
    recv, total, targets, codes = pl.pallas_call(
        exchange_kernel,
        out_shape=(
            jax.ShapeDtypeStruct((slots, SLOT, DIM), BF16),
            jax.ShapeDtypeStruct((LEAVES, RHS, LEAF), F32),
            jax.ShapeDtypeStruct((LEAVES, 2 * DIM, LEAF), BF16),
            jax.ShapeDtypeStruct((8, 128), I32),
        ),
        in_specs=[vmem, vmem, vmem, smem, hbm, vmem, hbm, vmem, smem, vmem, vmem],
        out_specs=(hbm, vmem, vmem, vmem),
        scratch_shapes=[
            pltpu.VMEM((LEAVES, LEAF, SKEL), BF16),
            pltpu.VMEM((LEAVES * SKEL, SKEL), BF16),
            pltpu.VMEM((LEAVES, DIM), I32),
            pltpu.VMEM((N_SUB, LEAVES, DIM), I32),
            pltpu.VMEM((LEAVES, PACKED, DIM), BF16),
            pltpu.VMEM((N_SUB, 2, SLOT, DIM), BF16),
            pltpu.VMEM((LEAVES, LEAF, DIM), BF16),
            pltpu.VMEM((LEAVES, DIM, SKEL), BF16),
            pltpu.VMEM((4, 4, HALF, DIM), BF16),
            pltpu.VMEM((4, 4, HALF, DIM), BF16),
            pltpu.VMEM((SKEL, 2 * DIM), F32),
            pltpu.VMEM((N_SUB, SKEL // N_SUB, 2 * DIM), F32),
            pltpu.VMEM((SKEL, 2 * DIM), BF16),
            pltpu.VMEM((N_LEAF - 1, SKEL, 2 * DIM), BF16),
            pltpu.VMEM((2 * EARLY, SLOT, DIM), BF16),
            pltpu.VMEM((2 * MIDDLE, SLOT, DIM), BF16),
            pltpu.VMEM((2 * MIDDLE, LEAF, DIM), BF16),
            pltpu.SMEM((8, 128), I32),
            dma((5,)),
            dma((N_SUB,)), dma((N_SUB,)),
            dma((N_SUB, 2)), dma((N_SUB, 2)),
            dma((2, 4)), dma((2, 4)), dma((2, 4)), dma((2, 4)),
            dma((N_SUB,)), dma((N_SUB,)),
            dma((N_SUB,)), dma((N_SUB,)),
            dma((N_LEAF - 1,)), dma((N_LEAF - 1,)),
        ],
        compiler_params=pltpu.CompilerParams(
            collective_id=0, has_side_effects=True, vmem_limit_bytes=56 << 20
        ),
    )(
        points.reshape(LEAVES, LEAF, DIM), charges.T, near_leaves, near_leaves,
        leaf_interpolant, skel_leaf, interp_mid[0], skel_mid, mid_partners, interp_top[0], skel_top,
    )
    out = pl.pallas_call(
        near_kernel,
        out_shape=jax.ShapeDtypeStruct((RHS, LEAVES * LEAF), F32),
        in_specs=[smem, hbm, vmem, vmem],
        out_specs=vmem,
        scratch_shapes=[
            pltpu.VMEM((slots, SLOT, DIM), BF16),
            pltpu.VMEM((slots, LEAF, DIM), BF16),
            pltpu.SMEM((STAGE,), I32),
            dma((slots,)),
        ],
        compiler_params=pltpu.CompilerParams(vmem_limit_bytes=56 << 20),
    )(codes, recv, targets, total)
    return out.T


def solution(mesh):
    placed = (
        P(("leaf", "sub"), None),
        P(("leaf", "sub"), None),
        P(("leaf", "sub"), None),
        P(("leaf", "sub"), None, None),
        P(("leaf", "sub"), None),
        P(("leaf", "sub"), None, None),
        P(("leaf", "sub"), None),
        P(("leaf", "sub"), None),
        P("leaf", "sub", None),
        P("leaf", None),
    )
    return jax.shard_map(
        body, mesh=mesh, in_specs=placed, out_specs=P(("leaf", "sub"), None), check_vma=False
    )
```

```python
import jax
import jax.numpy as jnp
from jax import lax
from jax.experimental import pallas as pl
from jax.experimental.pallas import tpu as pltpu
from jax.sharding import PartitionSpec as P

F32, BF16, I32 = jnp.float32, jnp.bfloat16, jnp.int32
MESH = pl.DeviceIdType.MESH

RATE = 0.5 * 1.4426950408889634

N_SUB, N_LEAF = 16, 8
LEAVES, LEAF, DIM, RHS, SKEL, NEAR = 8, 512, 128, 64, 256, 12
PACKED = RHS * LEAF // DIM
SLOT = LEAF + PACKED
MID = SKEL + RHS * SKEL // DIM
HALF = MID // 2

GROUPS = ((6, 12), (4, 14), (9, 3), (1, 11), (10,), (5, 15), (7, 13), (2, 8))
WINDOW = 5
ORDER = [k for ks in GROUPS for k in ks]
EARLY, MIDDLE = 8, 13
STAGE = 64


def dot(a, b):
    return jnp.dot(a, b, preferred_element_type=F32)


def dot_nt(a, b):
    return lax.dot_general(a, b, (((1,), (1,)), ((), ())), preferred_element_type=F32)


def pieces(x):
    hi = x.astype(BF16).astype(F32)
    mid = (x - hi).astype(BF16).astype(F32)
    return hi, mid, x - hi - mid


def source_side(rows):
    wide = rows.astype(F32)
    square = wide * wide
    high = square.astype(BF16)
    low = (square - high.astype(F32)).astype(BF16)
    half = jnp.full((2 * DIM, DIM), 0.5, BF16)
    hi, mid, lo = pieces(dot(jnp.concatenate((high, low), axis=1), half))
    lane = lax.broadcasted_iota(I32, hi.shape, 1)
    tail = jnp.where(lane < 6, 1.0, 0.0)
    return jnp.where(lane == 0, hi, jnp.where(lane == 1, mid, jnp.where(lane == 2, lo, tail))).astype(BF16)


def target_side(columns):
    wide = columns.astype(F32)
    half = 0.5 * jnp.sum(wide * wide, axis=0, keepdims=True)
    hi, mid, lo = pieces(half)
    row = lax.broadcasted_iota(I32, (16, columns.shape[1]), 0)
    head = jnp.where(row < 3, -1.0, 0.0)
    made = jnp.where(row == 3, -hi, jnp.where(row == 4, -mid, jnp.where(row == 5, -lo, head)))
    return jnp.concatenate((columns, made.astype(BF16), jnp.zeros((DIM - 16, columns.shape[1]), BF16)), axis=0)


def weighted(sources, weights, targets):
    kernel = jnp.exp2(dot(sources, targets) * RATE).astype(BF16)
    return dot(weights, kernel)


def unpacked(block):
    rows = block.shape[0] // RHS
    return jnp.concatenate([block[c * RHS : (c + 1) * RHS] for c in range(rows)], axis=1)


def packed(wide):
    return jnp.concatenate([wide[:, c : c + DIM] for c in range(0, wide.shape[1], DIM)], axis=0)


def sorted_lists(lists, first_leaf, z, y):
    shape = (128, 128)
    sub, lane = lax.broadcasted_iota(I32, shape, 0), lax.broadcasted_iota(I32, shape, 1)

    def down(row):
        return jnp.transpose(jnp.broadcast_to(row.astype(F32), shape)).astype(I32)

    tall = jnp.concatenate([jnp.broadcast_to(lists[l : l + 1, :], (16, 128)) for l in range(LEAVES)], axis=0)
    mine = jnp.where((sub % 16 == lane) & (sub % 16 < NEAR), tall - first_leaf, 0)
    column = jnp.broadcast_to(jnp.sum(mine.astype(F32), axis=1, keepdims=True), shape)
    va, vb = column.astype(I32), jnp.transpose(column).astype(I32)
    before = (sub % 16 < NEAR) & (va // LEAVES == vb // LEAVES) & (va < vb)
    slot = jnp.max(jnp.where(before, 1.0, 0.0), axis=0, keepdims=True).astype(I32)
    owner, place = vb[:1] // LEAVES, lane[:1] % 16
    shift = (z + 4 - owner // 4) % 4 * 4 + (y + 4 - owner % 4) % 4
    turn = jnp.zeros_like(shift)
    for at, k in enumerate(ORDER):
        turn = jnp.where(shift == k, at, turn)
    stage = jnp.where(turn < EARLY, 0, jnp.where(turn < MIDDLE, 1, 2))
    stage = jnp.where(place < NEAR, jnp.where(shift == 0, 3, stage), 4)
    key, code = stage * 16 + place, stage * STAGE + 2 * turn + slot
    same = sub // 16 == lane // 16
    rank = jnp.sum(jnp.where(same & (down(key) < key), 1.0, 0.0), axis=0, keepdims=True).astype(I32)
    chosen = jnp.where(same & (down(rank) == lane % 16), down(code), 0)
    return jnp.sum(chosen.astype(F32), axis=0, keepdims=True).astype(I32)


def progress(codes, l):
    first = both = remote = jnp.int32(0)
    for e in range(NEAR):
        code = codes[0, l * 16 + e]
        first += jnp.where(code < STAGE, 1, 0)
        both += jnp.where(code < 2 * STAGE, 1, 0)
        remote += jnp.where(code < 3 * STAGE, 1, 0)
    first = jnp.minimum(first, 4)
    return first, first + jnp.minimum(both - first, 4), remote


def listed_pairs(codes, l, start, width, limit, held, side, target):
    rows, weights = [], []
    spare = jnp.where(codes[0, l * 16 + start] < limit, codes[0, l * 16 + start], 0)
    for u in range(width):
        code = codes[0, l * 16 + start + u]
        real = code < limit
        slot = jnp.clip(jnp.where(real, code, spare) % STAGE, 0, held.shape[0] - 1)
        rows.append(jnp.concatenate((held[slot, :LEAF, :], side[slot]), axis=1))
        flag = jnp.where(real, 1.0, 0.0)
        weights.append((unpacked(held[slot, LEAF:, :]).astype(F32) * flag).astype(BF16))
    return weighted(jnp.concatenate(rows, axis=0), jnp.concatenate(weights, axis=1), target)


def exchange_kernel(
    points, charges, near, near_smem, interp_hbm, skel_leaf, mid_hbm, skel_mid, partners, top, skel_top,
    recv, total, targets, codes_out,
    interp, interp_mid, lists, list_in, charge_pack, send, own_side, skel_cols,
    mid_a, mid_b, scatter, scatter_in, gathered, crossed, early, held, side, codes,
    local_sem, list_s, list_r, near_s, near_r, ma_s, ma_r, mb_s, mb_r, sc_s, sc_r, ga_s, ga_r, cr_s, cr_r,
):
    me, group = lax.axis_index("sub"), lax.axis_index("leaf")
    z, y = me // 4, me % 4
    base = (group * N_SUB + me) * LEAVES

    def peer(k):
        return ((z + k // 4) % 4) * 4 + (y + k % 4) % 4

    def remote(src, dst, s, r, to):
        return pltpu.make_async_remote_copy(
            src_ref=src, dst_ref=dst, send_sem=s, recv_sem=r, device_id=to, device_id_type=MESH
        )

    def in_sub(src, dst, s, r, k):
        return remote(src, dst, s, r, (group, peer(k)))

    load_interp = pltpu.make_async_copy(interp_hbm, interp, local_sem.at[0])
    load_mid = pltpu.make_async_copy(mid_hbm, interp_mid, local_sem.at[1])
    load_interp.start()
    load_mid.start()

    barrier = pltpu.get_barrier_semaphore()
    for k in range(1, N_SUB):
        pl.semaphore_signal(barrier, inc=1, device_id=(group, peer(k)), device_id_type=MESH)
    for j in range(1, N_LEAF):
        pl.semaphore_signal(barrier, inc=1, device_id=((group + j) % N_LEAF, me), device_id_type=MESH)
    lists[...] = jnp.full(lists.shape, -1, I32)
    lists[:, :NEAR] = near[...]
    pl.semaphore_wait(barrier, N_SUB + N_LEAF - 2)

    list_copies = [None] + [
        in_sub(lists, list_in.at[k], list_s.at[k], list_r.at[k], k) for k in range(1, N_SUB)
    ]
    order = ORDER
    for k in order:
        list_copies[k].start()

    @pl.loop(0, LEAVES)
    def _(l):
        charge_pack[l] = packed(charges[:, pl.ds(pl.multiple_of(l * LEAF, LEAF), LEAF)])

    chosen = {}
    arrivals = {}

    def near_step(ks, s):
        started = []
        for k in ks:
            if s == 0:
                back = (-(k // 4)) % 4 * 4 + (-k) % 4
                list_copies[back].wait_recv()
                here = list_in[back] - base
                inside = (here >= 0) & (here < LEAVES)
                chosen[k] = (
                    jnp.min(jnp.where(inside, here, LEAVES - 1)),
                    jnp.max(jnp.where(inside, here, 0)),
                )
            leaf = chosen[k][s]
            send[k, s, :LEAF, :] = points[leaf]
            send[k, s, LEAF:, :] = charge_pack[leaf]
            at = 2 * ORDER.index(k) + s
            if at < 2 * EARLY:
                landing = early.at[at]
            elif at < 2 * MIDDLE:
                landing = held.at[at]
            else:
                landing = recv.at[at]
            c = in_sub(send.at[k, s], landing, near_s.at[k, s], near_r.at[k, s], k)
            c.start()
            started.append(c)
            arrivals[at] = c
        return started

    first, second = [], []

    def mid_step(ds):
        started = []
        for d in ds:
            started += [in_sub(mid_a.at[0], mid_a.at[d], ma_s.at[1, d], ma_r.at[1, d], 4 * d),
                        in_sub(mid_b.at[0], mid_b.at[d], mb_s.at[1, d], mb_r.at[1, d], d)]
        if not second:
            for c in first:
                c.wait_recv()
        for c in started:
            c.start()
        second.extend(started)
        return started

    steps = [(near_step, (ks, s)) for ks in GROUPS for s in range(2)]
    steps[10:10] = [(mid_step, ((1, 3),)), (mid_step, ((2,),))]
    taken = []

    def advance():
        t = len(taken)
        if t >= len(steps):
            return
        if t >= WINDOW:
            for c in taken[t - WINDOW]:
                c.wait_send()
        step, args = steps[t]
        taken.append(step(*args))

    for _ in range(WINDOW):
        advance()

    codes_out[...] = jnp.broadcast_to(sorted_lists(lists, group * N_SUB * LEAVES, z, y), codes_out.shape)
    save_codes = pltpu.make_async_copy(codes_out, codes, local_sem.at[2])
    save_codes.start()

    load_interp.wait()
    load_mid.wait()
    up = jnp.zeros((RHS, SKEL), F32)
    rows_in_leaf = lax.broadcasted_iota(I32, (LEAF, SKEL), 0)

    def upward(l, up):
        columns = jnp.transpose(points[l])
        targets[l] = target_side(columns)
        picks = jnp.where(rows_in_leaf == skel_leaf[pl.ds(l, 1), :], 1.0, 0.0).astype(BF16)
        skel_cols[l] = dot(columns, picks).astype(BF16)
        leaf_up = dot(unpacked(charge_pack[l]), interp[l]).astype(BF16)
        return up + dot(leaf_up, interp_mid[pl.ds(pl.multiple_of(l * SKEL, SKEL), SKEL), :])

    up = lax.fori_loop(0, LEAVES, upward, up)
    mid_up = up.astype(BF16)

    def pick_mid(l, cols):
        row = lax.broadcasted_iota(I32, (SKEL, SKEL), 0) + l * SKEL
        picks = jnp.where(row == skel_mid[...], 1.0, 0.0).astype(BF16)
        return cols + dot(skel_cols[l], picks)

    mid_cols = lax.fori_loop(0, LEAVES, pick_mid, jnp.zeros((DIM, SKEL), F32))
    mid_rows = jnp.transpose(mid_cols).astype(BF16)
    own_mid = jnp.concatenate((mid_rows, packed(mid_up)), axis=0)
    mid_a[0, 0] = own_mid[:HALF]
    mid_b[0, 0] = own_mid[HALF:]
    for d in (1, 3, 2):
        first.append(in_sub(mid_a.at[0, 0], mid_a.at[0, d], ma_s.at[0, d], ma_r.at[0, d], d))
        first.append(in_sub(mid_b.at[0, 0], mid_b.at[0, d], mb_s.at[0, d], mb_r.at[0, d], 4 * d))
    for c in first:
        c.start()

    row = lax.broadcasted_iota(I32, (SKEL, SKEL), 0) + me * SKEL
    picks = jnp.where(row == skel_top[...], 1.0, 0.0).astype(BF16)
    top_part = jnp.concatenate((dot(mid_up, top[...]), jnp.zeros((DIM - RHS, SKEL), F32)), axis=0)
    scatter[:, :DIM] = jnp.transpose(top_part)
    scatter[:, DIM:] = jnp.transpose(dot(mid_cols.astype(BF16), picks))
    piece = SKEL // N_SUB

    def rows_of(index):
        return pl.ds(pl.multiple_of(index * piece, piece), piece)

    scatter_copies = []
    for k in order:
        c = in_sub(scatter.at[rows_of(peer(k))], scatter_in.at[k], sc_s.at[k], sc_r.at[k], k)
        c.start()
        scatter_copies.append(c)
    advance()

    @pl.loop(0, LEAVES)
    def _(l):
        own_side[l] = source_side(points[l])

    def own_pairs(l):
        result = jnp.zeros((RHS, LEAF), F32)
        for part in range(0, LEAVES, 4):
            rows, weights = [], []
            for m in range(part, part + 4):
                named = near_smem[l, 0] == base + m
                for e in range(1, NEAR):
                    named = named | (near_smem[l, e] == base + m)
                flag = jnp.where(named, 1.0, 0.0)
                rows.append(jnp.concatenate((points[m], own_side[m]), axis=1))
                weights.append((unpacked(charge_pack[m]).astype(F32) * flag).astype(BF16))
            result += weighted(jnp.concatenate(rows, axis=0), jnp.concatenate(weights, axis=1), targets[l])
        total[l] = result

    def own_chunk(begin, end):
        pl.loop(begin, end)(own_pairs)

    own_chunk(0, 2)
    advance()
    own_chunk(2, 4)
    advance()

    for c in scatter_copies:
        c.wait_recv()
    summed = scatter[rows_of(me), :]
    for k in range(1, N_SUB):
        summed = summed + scatter_in[k]
    gathered[rows_of(me), :] = summed.astype(BF16)
    gather_copies = []
    for k in order:
        c = in_sub(gathered.at[rows_of(me)], gathered.at[rows_of(me)], ga_s.at[k], ga_r.at[k], k)
        c.start()
        gather_copies.append(c)

    advance()
    own_chunk(4, 6)
    advance()
    own_chunk(6, 8)
    advance()

    save_codes.wait()

    def arrived(begin, end):
        for at in range(2 * begin, 2 * end):
            arrivals[at].wait_recv()

    arrived(0, EARLY)
    keep_early = pltpu.make_async_copy(early, held.at[pl.ds(0, 2 * EARLY)], local_sem.at[3])
    keep_early.start()

    @pl.loop(0, 2 * EARLY)
    def _(i):
        side[i] = source_side(early[i, :LEAF, :])

    advance()

    def first_pass(l):
        total[l] += listed_pairs(codes, l, 0, 4, STAGE, early, side, targets[l])

    for begin in range(0, LEAVES, 2):
        pl.loop(begin, begin + 2)(first_pass)
        advance()
        if begin == 2:
            for c in gather_copies:
                c.wait_recv()
            cross_copies = []
            for j in (1, 7, 2, 6, 3, 5, 4):
                c = remote(gathered, crossed.at[j - 1], cr_s.at[j - 1], cr_r.at[j - 1], ((group + j) % N_LEAF, me))
                c.start()
                cross_copies.append(c)
    while len(taken) < len(steps):
        advance()

    for c in second:
        c.wait_recv()
    mid_targets = target_side(mid_cols.astype(BF16))
    rows, weights = [], []
    for p in range(4):
        node = partners[0, p] - group * N_SUB
        dz, dy = (z + 4 - node // 4) % 4, (y + 4 - node % 4) % 4
        block = jnp.concatenate((mid_a[dz, dy], mid_b[dy, dz]), axis=0)
        rows.append(jnp.concatenate((block[:SKEL], source_side(block[:SKEL])), axis=1))
        weights.append(unpacked(block[SKEL:]))
    mid_sum = weighted(jnp.concatenate(rows, axis=0), jnp.concatenate(weights, axis=1), mid_targets)

    for c in cross_copies:
        c.wait_recv()
    top_targets = target_side(jnp.transpose(gathered[:, DIM:].astype(F32)).astype(BF16))

    def top_from(j, acc):
        rows = crossed[j, :, DIM:]
        weights = jnp.transpose(crossed[j, :, :DIM].astype(F32)).astype(BF16)[:RHS]
        return acc + weighted(jnp.concatenate((rows, source_side(rows)), axis=1), weights, top_targets)

    top_sum = lax.fori_loop(0, N_LEAF - 1, top_from, jnp.zeros((RHS, SKEL), F32)).astype(BF16)
    mid_total = (mid_sum + dot_nt(top_sum, top[...])).astype(BF16)

    @pl.loop(0, LEAVES)
    def _(l):
        down = dot_nt(mid_total, interp_mid[pl.ds(pl.multiple_of(l * SKEL, SKEL), SKEL), :]).astype(BF16)
        total[l] += dot_nt(down, interp[l])

    keep_early.wait()
    arrived(EARLY, MIDDLE)
    keep_held = pltpu.make_async_copy(held, recv.at[pl.ds(0, 2 * MIDDLE)], local_sem.at[4])
    keep_held.start()

    @pl.loop(2 * EARLY, 2 * MIDDLE)
    def _(i):
        side[i] = source_side(held[i, :LEAF, :])

    @pl.loop(0, LEAVES)
    def _(l):
        start, _, _ = progress(codes, l)
        total[l] += listed_pairs(codes, l, start, 4, 2 * STAGE, held, side, targets[l])

    for copies in taken[len(steps) - WINDOW :]:
        for c in copies:
            c.wait_send()
    for c in list_copies[1:] + first + scatter_copies + gather_copies + cross_copies:
        c.wait_send()
    keep_held.wait()
    arrived(MIDDLE, N_SUB - 1)


def near_kernel(codes, recv, targets, total, out, held, side, used, sem):
    slots = held.shape[0]
    for i in range(STAGE):
        used[i] = 0

    @pl.loop(0, LEAVES)
    def _(l):
        _, begin, end = progress(codes, l)
        for e in range(NEAR):
            slot = codes[0, l * 16 + e] % STAGE
            used[slot] = jnp.maximum(used[slot], jnp.where((begin <= e) & (e < end), 1, 0))

    def copy(i):
        return pltpu.make_async_copy(recv.at[i], held.at[i], sem.at[i])

    @pl.loop(0, slots)
    def _(i):
        pl.when(used[i] > 0)(lambda: copy(i).start())

    @pl.loop(0, slots)
    def _(i):
        @pl.when(used[i] > 0)
        def _():
            copy(i).wait()
            side[i] = source_side(held[i, :LEAF, :])

    @pl.loop(0, LEAVES)
    def _(l):
        _, begin, end = progress(codes, l)

        def two(n, acc):
            return acc + listed_pairs(codes, l, begin + 2 * n, 2, 3 * STAGE, held, side, targets[l])

        acc = lax.fori_loop(0, (end - begin + 1) // 2, two, total[l])
        out[:, pl.ds(pl.multiple_of(l * LEAF, LEAF), LEAF)] = acc


def body(
    points, charges, near_leaves, leaf_interpolant, skel_leaf,
    interp_mid, skel_mid, mid_partners, interp_top, skel_top,
):
    vmem, smem, hbm = (pl.BlockSpec(memory_space=m) for m in (pltpu.VMEM, pltpu.SMEM, pl.ANY))
    dma = pltpu.SemaphoreType.DMA
    slots = 2 * (N_SUB - 1)
    recv, total, targets, codes = pl.pallas_call(
        exchange_kernel,
        out_shape=(
            jax.ShapeDtypeStruct((slots, SLOT, DIM), BF16),
            jax.ShapeDtypeStruct((LEAVES, RHS, LEAF), F32),
            jax.ShapeDtypeStruct((LEAVES, 2 * DIM, LEAF), BF16),
            jax.ShapeDtypeStruct((8, 128), I32),
        ),
        in_specs=[vmem, vmem, vmem, smem, hbm, vmem, hbm, vmem, smem, vmem, vmem],
        out_specs=(hbm, vmem, vmem, vmem),
        scratch_shapes=[
            pltpu.VMEM((LEAVES, LEAF, SKEL), BF16),
            pltpu.VMEM((LEAVES * SKEL, SKEL), BF16),
            pltpu.VMEM((LEAVES, DIM), I32),
            pltpu.VMEM((N_SUB, LEAVES, DIM), I32),
            pltpu.VMEM((LEAVES, PACKED, DIM), BF16),
            pltpu.VMEM((N_SUB, 2, SLOT, DIM), BF16),
            pltpu.VMEM((LEAVES, LEAF, DIM), BF16),
            pltpu.VMEM((LEAVES, DIM, SKEL), BF16),
            pltpu.VMEM((4, 4, HALF, DIM), BF16),
            pltpu.VMEM((4, 4, HALF, DIM), BF16),
            pltpu.VMEM((SKEL, 2 * DIM), F32),
            pltpu.VMEM((N_SUB, SKEL // N_SUB, 2 * DIM), F32),
            pltpu.VMEM((SKEL, 2 * DIM), BF16),
            pltpu.VMEM((N_LEAF - 1, SKEL, 2 * DIM), BF16),
            pltpu.VMEM((2 * EARLY, SLOT, DIM), BF16),
            pltpu.VMEM((2 * MIDDLE, SLOT, DIM), BF16),
            pltpu.VMEM((2 * MIDDLE, LEAF, DIM), BF16),
            pltpu.SMEM((8, 128), I32),
            dma((5,)),
            dma((N_SUB,)), dma((N_SUB,)),
            dma((N_SUB, 2)), dma((N_SUB, 2)),
            dma((2, 4)), dma((2, 4)), dma((2, 4)), dma((2, 4)),
            dma((N_SUB,)), dma((N_SUB,)),
            dma((N_SUB,)), dma((N_SUB,)),
            dma((N_LEAF - 1,)), dma((N_LEAF - 1,)),
        ],
        compiler_params=pltpu.CompilerParams(
            collective_id=0, has_side_effects=True, vmem_limit_bytes=56 << 20
        ),
    )(
        points.reshape(LEAVES, LEAF, DIM), charges.T, near_leaves, near_leaves,
        leaf_interpolant, skel_leaf, interp_mid[0], skel_mid, mid_partners, interp_top[0], skel_top,
    )
    out = pl.pallas_call(
        near_kernel,
        out_shape=jax.ShapeDtypeStruct((RHS, LEAVES * LEAF), F32),
        in_specs=[smem, hbm, vmem, vmem],
        out_specs=vmem,
        scratch_shapes=[
            pltpu.VMEM((slots, SLOT, DIM), BF16),
            pltpu.VMEM((slots, LEAF, DIM), BF16),
            pltpu.SMEM((STAGE,), I32),
            dma((slots,)),
        ],
        compiler_params=pltpu.CompilerParams(vmem_limit_bytes=56 << 20),
    )(codes, recv, targets, total)
    return out.T


def solution(mesh):
    placed = (
        P(("leaf", "sub"), None),
        P(("leaf", "sub"), None),
        P(("leaf", "sub"), None),
        P(("leaf", "sub"), None, None),
        P(("leaf", "sub"), None),
        P(("leaf", "sub"), None, None),
        P(("leaf", "sub"), None),
        P(("leaf", "sub"), None),
        P("leaf", "sub", None),
        P("leaf", None),
    )
    return jax.shard_map(
        body, mesh=mesh, in_specs=placed, out_specs=P(("leaf", "sub"), None), check_vma=False
    )
```

```python
import jax
import jax.numpy as jnp
from jax import lax
from jax.experimental import pallas as pl
from jax.experimental.pallas import tpu as pltpu
from jax.sharding import PartitionSpec as P

F32, BF16, I32 = jnp.float32, jnp.bfloat16, jnp.int32
MESH = pl.DeviceIdType.MESH

RATE = 0.5 * 1.4426950408889634

N_SUB, N_LEAF = 16, 8
LEAVES, LEAF, DIM, RHS, SKEL, NEAR = 8, 512, 128, 64, 256, 12
PACKED = RHS * LEAF // DIM
SLOT = LEAF + PACKED
MID = SKEL + RHS * SKEL // DIM
HALF = MID // 2

GROUPS = ((6, 12), (4, 14), (9, 3), (1, 11), (10,), (5, 15), (7, 13), (2, 8))
WINDOW = 5
ORDER = [k for ks in GROUPS for k in ks]
EARLY, MIDDLE = 8, 11
STAGE = 64


def dot(a, b):
    return jnp.dot(a, b, preferred_element_type=F32)


def dot_nt(a, b):
    return lax.dot_general(a, b, (((1,), (1,)), ((), ())), preferred_element_type=F32)


def pieces(x):
    hi = x.astype(BF16).astype(F32)
    mid = (x - hi).astype(BF16).astype(F32)
    return hi, mid, x - hi - mid


def source_side(rows):
    wide = rows.astype(F32)
    square = wide * wide
    high = square.astype(BF16)
    low = (square - high.astype(F32)).astype(BF16)
    half = jnp.full((2 * DIM, DIM), 0.5, BF16)
    hi, mid, lo = pieces(dot(jnp.concatenate((high, low), axis=1), half))
    lane = lax.broadcasted_iota(I32, hi.shape, 1)
    tail = jnp.where(lane < 6, 1.0, 0.0)
    return jnp.where(lane == 0, hi, jnp.where(lane == 1, mid, jnp.where(lane == 2, lo, tail))).astype(BF16)


def target_side(columns):
    wide = columns.astype(F32)
    half = 0.5 * jnp.sum(wide * wide, axis=0, keepdims=True)
    hi, mid, lo = pieces(half)
    row = lax.broadcasted_iota(I32, (16, columns.shape[1]), 0)
    head = jnp.where(row < 3, -1.0, 0.0)
    made = jnp.where(row == 3, -hi, jnp.where(row == 4, -mid, jnp.where(row == 5, -lo, head)))
    return jnp.concatenate((columns, made.astype(BF16), jnp.zeros((DIM - 16, columns.shape[1]), BF16)), axis=0)


def weighted(sources, weights, targets):
    kernel = jnp.exp2(dot(sources, targets) * RATE).astype(BF16)
    return dot(weights, kernel)


def unpacked(block):
    rows = block.shape[0] // RHS
    return jnp.concatenate([block[c * RHS : (c + 1) * RHS] for c in range(rows)], axis=1)


def packed(wide):
    return jnp.concatenate([wide[:, c : c + DIM] for c in range(0, wide.shape[1], DIM)], axis=0)


def sorted_lists(lists, first_leaf, z, y):
    shape = (128, 128)
    sub, lane = lax.broadcasted_iota(I32, shape, 0), lax.broadcasted_iota(I32, shape, 1)

    def down(row):
        return jnp.transpose(jnp.broadcast_to(row.astype(F32), shape)).astype(I32)

    tall = jnp.concatenate([jnp.broadcast_to(lists[l : l + 1, :], (16, 128)) for l in range(LEAVES)], axis=0)
    mine = jnp.where((sub % 16 == lane) & (sub % 16 < NEAR), tall - first_leaf, 0)
    column = jnp.broadcast_to(jnp.sum(mine.astype(F32), axis=1, keepdims=True), shape)
    va, vb = column.astype(I32), jnp.transpose(column).astype(I32)
    before = (sub % 16 < NEAR) & (va // LEAVES == vb // LEAVES) & (va < vb)
    slot = jnp.max(jnp.where(before, 1.0, 0.0), axis=0, keepdims=True).astype(I32)
    owner, place = vb[:1] // LEAVES, lane[:1] % 16
    shift = (z + 4 - owner // 4) % 4 * 4 + (y + 4 - owner % 4) % 4
    turn = jnp.zeros_like(shift)
    for at, k in enumerate(ORDER):
        turn = jnp.where(shift == k, at, turn)
    stage = jnp.where(turn < EARLY, 0, jnp.where(turn < MIDDLE, 1, 2))
    stage = jnp.where(place < NEAR, jnp.where(shift == 0, 3, stage), 4)
    key, code = stage * 16 + place, stage * STAGE + 2 * turn + slot
    same = sub // 16 == lane // 16
    rank = jnp.sum(jnp.where(same & (down(key) < key), 1.0, 0.0), axis=0, keepdims=True).astype(I32)
    chosen = jnp.where(same & (down(rank) == lane % 16), down(code), 0)
    return jnp.sum(chosen.astype(F32), axis=0, keepdims=True).astype(I32)


def progress(codes, l):
    first = both = remote = jnp.int32(0)
    for e in range(NEAR):
        code = codes[0, l * 16 + e]
        first += jnp.where(code < STAGE, 1, 0)
        both += jnp.where(code < 2 * STAGE, 1, 0)
        remote += jnp.where(code < 3 * STAGE, 1, 0)
    first = jnp.minimum(first, 4)
    return first, first + jnp.minimum(both - first, 4), remote


def listed_pairs(codes, l, start, width, limit, held, side, target):
    rows, weights = [], []
    spare = jnp.where(codes[0, l * 16 + start] < limit, codes[0, l * 16 + start], 0)
    for u in range(width):
        code = codes[0, l * 16 + start + u]
        real = code < limit
        slot = jnp.clip(jnp.where(real, code, spare) % STAGE, 0, held.shape[0] - 1)
        rows.append(jnp.concatenate((held[slot, :LEAF, :], side[slot]), axis=1))
        flag = jnp.where(real, 1.0, 0.0)
        weights.append((unpacked(held[slot, LEAF:, :]).astype(F32) * flag).astype(BF16))
    return weighted(jnp.concatenate(rows, axis=0), jnp.concatenate(weights, axis=1), target)


def exchange_kernel(
    points, charges, near, near_smem, interp_hbm, skel_leaf, mid_hbm, skel_mid, partners, top, skel_top,
    recv, total, targets, codes_out,
    interp, interp_mid, lists, list_in, charge_pack, send, own_side, skel_cols,
    mid_a, mid_b, scatter, scatter_in, gathered, crossed, early, held, side, codes,
    local_sem, list_s, list_r, near_s, near_r, ma_s, ma_r, mb_s, mb_r, sc_s, sc_r, ga_s, ga_r, cr_s, cr_r,
):
    me, group = lax.axis_index("sub"), lax.axis_index("leaf")
    z, y = me // 4, me % 4
    base = (group * N_SUB + me) * LEAVES

    def peer(k):
        return ((z + k // 4) % 4) * 4 + (y + k % 4) % 4

    def remote(src, dst, s, r, to):
        return pltpu.make_async_remote_copy(
            src_ref=src, dst_ref=dst, send_sem=s, recv_sem=r, device_id=to, device_id_type=MESH
        )

    def in_sub(src, dst, s, r, k):
        return remote(src, dst, s, r, (group, peer(k)))

    load_interp = pltpu.make_async_copy(interp_hbm, interp, local_sem.at[0])
    load_mid = pltpu.make_async_copy(mid_hbm, interp_mid, local_sem.at[1])
    load_interp.start()
    load_mid.start()

    barrier = pltpu.get_barrier_semaphore()
    for k in range(1, N_SUB):
        pl.semaphore_signal(barrier, inc=1, device_id=(group, peer(k)), device_id_type=MESH)
    for j in range(1, N_LEAF):
        pl.semaphore_signal(barrier, inc=1, device_id=((group + j) % N_LEAF, me), device_id_type=MESH)
    lists[...] = jnp.full(lists.shape, -1, I32)
    lists[:, :NEAR] = near[...]
    pl.semaphore_wait(barrier, N_SUB + N_LEAF - 2)

    list_copies = [None] + [
        in_sub(lists, list_in.at[k], list_s.at[k], list_r.at[k], k) for k in range(1, N_SUB)
    ]
    order = ORDER
    for k in order:
        list_copies[k].start()

    @pl.loop(0, LEAVES)
    def _(l):
        charge_pack[l] = packed(charges[:, pl.ds(pl.multiple_of(l * LEAF, LEAF), LEAF)])

    chosen = {}
    arrivals = {}

    def near_step(ks, s):
        started = []
        for k in ks:
            if s == 0:
                back = (-(k // 4)) % 4 * 4 + (-k) % 4
                list_copies[back].wait_recv()
                here = list_in[back] - base
                inside = (here >= 0) & (here < LEAVES)
                chosen[k] = (
                    jnp.min(jnp.where(inside, here, LEAVES - 1)),
                    jnp.max(jnp.where(inside, here, 0)),
                )
            leaf = chosen[k][s]
            send[k, s, :LEAF, :] = points[leaf]
            send[k, s, LEAF:, :] = charge_pack[leaf]
            at = 2 * ORDER.index(k) + s
            if at < 2 * EARLY:
                landing = early.at[at]
            elif at < 2 * MIDDLE:
                landing = held.at[at]
            else:
                landing = recv.at[at]
            c = in_sub(send.at[k, s], landing, near_s.at[k, s], near_r.at[k, s], k)
            c.start()
            started.append(c)
            arrivals[at] = c
        return started

    first, second = [], []

    def mid_step(ds):
        started = []
        for d in ds:
            started += [in_sub(mid_a.at[0], mid_a.at[d], ma_s.at[1, d], ma_r.at[1, d], 4 * d),
                        in_sub(mid_b.at[0], mid_b.at[d], mb_s.at[1, d], mb_r.at[1, d], d)]
        if not second:
            for c in first:
                c.wait_recv()
        for c in started:
            c.start()
        second.extend(started)
        return started

    steps = [(near_step, (ks, s)) for ks in GROUPS for s in range(2)]
    steps[10:10] = [(mid_step, ((1, 3),)), (mid_step, ((2,),))]
    taken = []

    def advance():
        t = len(taken)
        if t >= len(steps):
            return
        if t >= WINDOW:
            for c in taken[t - WINDOW]:
                c.wait_send()
        step, args = steps[t]
        taken.append(step(*args))

    for _ in range(WINDOW):
        advance()

    codes_out[...] = jnp.broadcast_to(sorted_lists(lists, group * N_SUB * LEAVES, z, y), codes_out.shape)
    save_codes = pltpu.make_async_copy(codes_out, codes, local_sem.at[2])
    save_codes.start()

    load_interp.wait()
    load_mid.wait()
    up = jnp.zeros((RHS, SKEL), F32)
    rows_in_leaf = lax.broadcasted_iota(I32, (LEAF, SKEL), 0)

    def upward(l, up):
        columns = jnp.transpose(points[l])
        targets[l] = target_side(columns)
        picks = jnp.where(rows_in_leaf == skel_leaf[pl.ds(l, 1), :], 1.0, 0.0).astype(BF16)
        skel_cols[l] = dot(columns, picks).astype(BF16)
        leaf_up = dot(unpacked(charge_pack[l]), interp[l]).astype(BF16)
        return up + dot(leaf_up, interp_mid[pl.ds(pl.multiple_of(l * SKEL, SKEL), SKEL), :])

    up = lax.fori_loop(0, LEAVES, upward, up)
    mid_up = up.astype(BF16)

    def pick_mid(l, cols):
        row = lax.broadcasted_iota(I32, (SKEL, SKEL), 0) + l * SKEL
        picks = jnp.where(row == skel_mid[...], 1.0, 0.0).astype(BF16)
        return cols + dot(skel_cols[l], picks)

    mid_cols = lax.fori_loop(0, LEAVES, pick_mid, jnp.zeros((DIM, SKEL), F32))
    mid_rows = jnp.transpose(mid_cols).astype(BF16)
    own_mid = jnp.concatenate((mid_rows, packed(mid_up)), axis=0)
    mid_a[0, 0] = own_mid[:HALF]
    mid_b[0, 0] = own_mid[HALF:]
    for d in (1, 3, 2):
        first.append(in_sub(mid_a.at[0, 0], mid_a.at[0, d], ma_s.at[0, d], ma_r.at[0, d], d))
        first.append(in_sub(mid_b.at[0, 0], mid_b.at[0, d], mb_s.at[0, d], mb_r.at[0, d], 4 * d))
    for c in first:
        c.start()

    row = lax.broadcasted_iota(I32, (SKEL, SKEL), 0) + me * SKEL
    picks = jnp.where(row == skel_top[...], 1.0, 0.0).astype(BF16)
    top_part = jnp.concatenate((dot(mid_up, top[...]), jnp.zeros((DIM - RHS, SKEL), F32)), axis=0)
    scatter[:, :DIM] = jnp.transpose(top_part)
    scatter[:, DIM:] = jnp.transpose(dot(mid_cols.astype(BF16), picks))
    piece = SKEL // N_SUB

    def rows_of(index):
        return pl.ds(pl.multiple_of(index * piece, piece), piece)

    scatter_copies = []
    for k in order:
        c = in_sub(scatter.at[rows_of(peer(k))], scatter_in.at[k], sc_s.at[k], sc_r.at[k], k)
        c.start()
        scatter_copies.append(c)
    advance()

    @pl.loop(0, LEAVES)
    def _(l):
        own_side[l] = source_side(points[l])

    def own_pairs(l):
        result = jnp.zeros((RHS, LEAF), F32)
        for part in range(0, LEAVES, 4):
            rows, weights = [], []
            for m in range(part, part + 4):
                named = near_smem[l, 0] == base + m
                for e in range(1, NEAR):
                    named = named | (near_smem[l, e] == base + m)
                flag = jnp.where(named, 1.0, 0.0)
                rows.append(jnp.concatenate((points[m], own_side[m]), axis=1))
                weights.append((unpacked(charge_pack[m]).astype(F32) * flag).astype(BF16))
            result += weighted(jnp.concatenate(rows, axis=0), jnp.concatenate(weights, axis=1), targets[l])
        total[l] = result

    def own_chunk(begin, end):
        pl.loop(begin, end)(own_pairs)

    own_chunk(0, 2)
    advance()
    own_chunk(2, 4)
    advance()

    for c in scatter_copies:
        c.wait_recv()
    summed = scatter[rows_of(me), :]
    for k in range(1, N_SUB):
        summed = summed + scatter_in[k]
    gathered[rows_of(me), :] = summed.astype(BF16)
    gather_copies = []
    for k in order:
        c = in_sub(gathered.at[rows_of(me)], gathered.at[rows_of(me)], ga_s.at[k], ga_r.at[k], k)
        c.start()
        gather_copies.append(c)

    advance()
    own_chunk(4, 6)
    advance()
    own_chunk(6, 8)
    advance()

    save_codes.wait()

    def arrived(begin, end):
        for at in range(2 * begin, 2 * end):
            arrivals[at].wait_recv()

    arrived(0, EARLY)
    keep_early = pltpu.make_async_copy(early, held.at[pl.ds(0, 2 * EARLY)], local_sem.at[3])
    keep_early.start()

    @pl.loop(0, 2 * EARLY)
    def _(i):
        side[i] = source_side(early[i, :LEAF, :])

    advance()

    def first_pass(l):
        total[l] += listed_pairs(codes, l, 0, 4, STAGE, early, side, targets[l])

    for begin in range(0, LEAVES, 2):
        pl.loop(begin, begin + 2)(first_pass)
        advance()
        if begin == 2:
            for c in gather_copies:
                c.wait_recv()
            cross_copies = []
            for j in (1, 7, 2, 6, 3, 5, 4):
                c = remote(gathered, crossed.at[j - 1], cr_s.at[j - 1], cr_r.at[j - 1], ((group + j) % N_LEAF, me))
                c.start()
                cross_copies.append(c)
    while len(taken) < len(steps):
        advance()

    for c in second:
        c.wait_recv()
    mid_targets = target_side(mid_cols.astype(BF16))
    rows, weights = [], []
    for p in range(4):
        node = partners[0, p] - group * N_SUB
        dz, dy = (z + 4 - node // 4) % 4, (y + 4 - node % 4) % 4
        block = jnp.concatenate((mid_a[dz, dy], mid_b[dy, dz]), axis=0)
        rows.append(jnp.concatenate((block[:SKEL], source_side(block[:SKEL])), axis=1))
        weights.append(unpacked(block[SKEL:]))
    mid_sum = weighted(jnp.concatenate(rows, axis=0), jnp.concatenate(weights, axis=1), mid_targets)

    for c in cross_copies:
        c.wait_recv()
    top_targets = target_side(jnp.transpose(gathered[:, DIM:].astype(F32)).astype(BF16))

    def top_from(j, acc):
        rows = crossed[j, :, DIM:]
        weights = jnp.transpose(crossed[j, :, :DIM].astype(F32)).astype(BF16)[:RHS]
        return acc + weighted(jnp.concatenate((rows, source_side(rows)), axis=1), weights, top_targets)

    top_sum = lax.fori_loop(0, N_LEAF - 1, top_from, jnp.zeros((RHS, SKEL), F32)).astype(BF16)
    mid_total = (mid_sum + dot_nt(top_sum, top[...])).astype(BF16)

    @pl.loop(0, LEAVES)
    def _(l):
        down = dot_nt(mid_total, interp_mid[pl.ds(pl.multiple_of(l * SKEL, SKEL), SKEL), :]).astype(BF16)
        total[l] += dot_nt(down, interp[l])

    keep_early.wait()
    arrived(EARLY, MIDDLE)
    keep_held = pltpu.make_async_copy(held, recv.at[pl.ds(0, 2 * MIDDLE)], local_sem.at[4])
    keep_held.start()

    @pl.loop(2 * EARLY, 2 * MIDDLE)
    def _(i):
        side[i] = source_side(held[i, :LEAF, :])

    @pl.loop(0, LEAVES)
    def _(l):
        start, _, _ = progress(codes, l)
        total[l] += listed_pairs(codes, l, start, 4, 2 * STAGE, held, side, targets[l])

    for copies in taken[len(steps) - WINDOW :]:
        for c in copies:
            c.wait_send()
    for c in list_copies[1:] + first + scatter_copies + gather_copies + cross_copies:
        c.wait_send()
    keep_held.wait()
    arrived(MIDDLE, N_SUB - 1)


def near_kernel(codes, recv, targets, total, out, held, side, used, sem):
    slots = held.shape[0]
    for i in range(STAGE):
        used[i] = 0

    @pl.loop(0, LEAVES)
    def _(l):
        _, begin, end = progress(codes, l)
        for e in range(NEAR):
            slot = codes[0, l * 16 + e] % STAGE
            used[slot] = jnp.maximum(used[slot], jnp.where((begin <= e) & (e < end), 1, 0))

    def copy(i):
        return pltpu.make_async_copy(recv.at[i], held.at[i], sem.at[i])

    @pl.loop(0, slots)
    def _(i):
        pl.when(used[i] > 0)(lambda: copy(i).start())

    @pl.loop(0, slots)
    def _(i):
        @pl.when(used[i] > 0)
        def _():
            copy(i).wait()
            side[i] = source_side(held[i, :LEAF, :])

    @pl.loop(0, LEAVES)
    def _(l):
        _, begin, end = progress(codes, l)

        def two(n, acc):
            return acc + listed_pairs(codes, l, begin + 2 * n, 2, 3 * STAGE, held, side, targets[l])

        acc = lax.fori_loop(0, (end - begin + 1) // 2, two, total[l])
        out[:, pl.ds(pl.multiple_of(l * LEAF, LEAF), LEAF)] = acc


def body(
    points, charges, near_leaves, leaf_interpolant, skel_leaf,
    interp_mid, skel_mid, mid_partners, interp_top, skel_top,
):
    vmem, smem, hbm = (pl.BlockSpec(memory_space=m) for m in (pltpu.VMEM, pltpu.SMEM, pl.ANY))
    dma = pltpu.SemaphoreType.DMA
    slots = 2 * (N_SUB - 1)
    recv, total, targets, codes = pl.pallas_call(
        exchange_kernel,
        out_shape=(
            jax.ShapeDtypeStruct((slots, SLOT, DIM), BF16),
            jax.ShapeDtypeStruct((LEAVES, RHS, LEAF), F32),
            jax.ShapeDtypeStruct((LEAVES, 2 * DIM, LEAF), BF16),
            jax.ShapeDtypeStruct((8, 128), I32),
        ),
        in_specs=[vmem, vmem, vmem, smem, hbm, vmem, hbm, vmem, smem, vmem, vmem],
        out_specs=(hbm, vmem, vmem, vmem),
        scratch_shapes=[
            pltpu.VMEM((LEAVES, LEAF, SKEL), BF16),
            pltpu.VMEM((LEAVES * SKEL, SKEL), BF16),
            pltpu.VMEM((LEAVES, DIM), I32),
            pltpu.VMEM((N_SUB, LEAVES, DIM), I32),
            pltpu.VMEM((LEAVES, PACKED, DIM), BF16),
            pltpu.VMEM((N_SUB, 2, SLOT, DIM), BF16),
            pltpu.VMEM((LEAVES, LEAF, DIM), BF16),
            pltpu.VMEM((LEAVES, DIM, SKEL), BF16),
            pltpu.VMEM((4, 4, HALF, DIM), BF16),
            pltpu.VMEM((4, 4, HALF, DIM), BF16),
            pltpu.VMEM((SKEL, 2 * DIM), F32),
            pltpu.VMEM((N_SUB, SKEL // N_SUB, 2 * DIM), F32),
            pltpu.VMEM((SKEL, 2 * DIM), BF16),
            pltpu.VMEM((N_LEAF - 1, SKEL, 2 * DIM), BF16),
            pltpu.VMEM((2 * EARLY, SLOT, DIM), BF16),
            pltpu.VMEM((2 * MIDDLE, SLOT, DIM), BF16),
            pltpu.VMEM((2 * MIDDLE, LEAF, DIM), BF16),
            pltpu.SMEM((8, 128), I32),
            dma((5,)),
            dma((N_SUB,)), dma((N_SUB,)),
            dma((N_SUB, 2)), dma((N_SUB, 2)),
            dma((2, 4)), dma((2, 4)), dma((2, 4)), dma((2, 4)),
            dma((N_SUB,)), dma((N_SUB,)),
            dma((N_SUB,)), dma((N_SUB,)),
            dma((N_LEAF - 1,)), dma((N_LEAF - 1,)),
        ],
        compiler_params=pltpu.CompilerParams(
            collective_id=0, has_side_effects=True, vmem_limit_bytes=56 << 20
        ),
    )(
        points.reshape(LEAVES, LEAF, DIM), charges.T, near_leaves, near_leaves,
        leaf_interpolant, skel_leaf, interp_mid[0], skel_mid, mid_partners, interp_top[0], skel_top,
    )
    out = pl.pallas_call(
        near_kernel,
        out_shape=jax.ShapeDtypeStruct((RHS, LEAVES * LEAF), F32),
        in_specs=[smem, hbm, vmem, vmem],
        out_specs=vmem,
        scratch_shapes=[
            pltpu.VMEM((slots, SLOT, DIM), BF16),
            pltpu.VMEM((slots, LEAF, DIM), BF16),
            pltpu.SMEM((STAGE,), I32),
            dma((slots,)),
        ],
        compiler_params=pltpu.CompilerParams(vmem_limit_bytes=56 << 20),
    )(codes, recv, targets, total)
    return out.T


def solution(mesh):
    placed = (
        P(("leaf", "sub"), None),
        P(("leaf", "sub"), None),
        P(("leaf", "sub"), None),
        P(("leaf", "sub"), None, None),
        P(("leaf", "sub"), None),
        P(("leaf", "sub"), None, None),
        P(("leaf", "sub"), None),
        P(("leaf", "sub"), None),
        P("leaf", "sub", None),
        P("leaf", None),
    )
    return jax.shard_map(
        body, mesh=mesh, in_specs=placed, out_specs=P(("leaf", "sub"), None), check_vma=False
    )
```

```python
import jax
import jax.numpy as jnp
from jax import lax
from jax.experimental import pallas as pl
from jax.experimental.pallas import tpu as pltpu
from jax.sharding import PartitionSpec as P

F32, BF16, I32 = jnp.float32, jnp.bfloat16, jnp.int32
MESH = pl.DeviceIdType.MESH

RATE = 0.5 * 1.4426950408889634

N_SUB, N_LEAF = 16, 8
LEAVES, LEAF, DIM, RHS, SKEL, NEAR = 8, 512, 128, 64, 256, 12
PACKED = RHS * LEAF // DIM
SLOT = LEAF + PACKED
MID = SKEL + RHS * SKEL // DIM
HALF = MID // 2

GROUPS = ((6, 12), (4, 14), (9, 3), (1, 11), (10,), (5, 15), (7, 13), (2, 8))
WINDOW = 5
ORDER = [k for ks in GROUPS for k in ks]
EARLY, MIDDLE = 8, 12
STAGE = 64


def dot(a, b):
    return jnp.dot(a, b, preferred_element_type=F32)


def dot_nt(a, b):
    return lax.dot_general(a, b, (((1,), (1,)), ((), ())), preferred_element_type=F32)


def pieces(x):
    hi = x.astype(BF16).astype(F32)
    mid = (x - hi).astype(BF16).astype(F32)
    return hi, mid, x - hi - mid


def source_side(rows):
    wide = rows.astype(F32)
    square = wide * wide
    high = square.astype(BF16)
    low = (square - high.astype(F32)).astype(BF16)
    half = jnp.full((2 * DIM, DIM), 0.5, BF16)
    hi, mid, lo = pieces(dot(jnp.concatenate((high, low), axis=1), half))
    lane = lax.broadcasted_iota(I32, hi.shape, 1)
    tail = jnp.where(lane < 6, 1.0, 0.0)
    return jnp.where(lane == 0, hi, jnp.where(lane == 1, mid, jnp.where(lane == 2, lo, tail))).astype(BF16)


def target_side(columns):
    wide = columns.astype(F32)
    half = 0.5 * jnp.sum(wide * wide, axis=0, keepdims=True)
    hi, mid, lo = pieces(half)
    row = lax.broadcasted_iota(I32, (16, columns.shape[1]), 0)
    head = jnp.where(row < 3, -1.0, 0.0)
    made = jnp.where(row == 3, -hi, jnp.where(row == 4, -mid, jnp.where(row == 5, -lo, head)))
    return jnp.concatenate((columns, made.astype(BF16), jnp.zeros((DIM - 16, columns.shape[1]), BF16)), axis=0)


def weighted(sources, weights, targets):
    kernel = jnp.exp2(dot(sources, targets) * RATE).astype(BF16)
    return dot(weights, kernel)


def unpacked(block):
    rows = block.shape[0] // RHS
    return jnp.concatenate([block[c * RHS : (c + 1) * RHS] for c in range(rows)], axis=1)


def packed(wide):
    return jnp.concatenate([wide[:, c : c + DIM] for c in range(0, wide.shape[1], DIM)], axis=0)


def sorted_lists(lists, first_leaf, z, y):
    shape = (128, 128)
    sub, lane = lax.broadcasted_iota(I32, shape, 0), lax.broadcasted_iota(I32, shape, 1)

    def down(row):
        return jnp.transpose(jnp.broadcast_to(row.astype(F32), shape)).astype(I32)

    tall = jnp.concatenate([jnp.broadcast_to(lists[l : l + 1, :], (16, 128)) for l in range(LEAVES)], axis=0)
    mine = jnp.where((sub % 16 == lane) & (sub % 16 < NEAR), tall - first_leaf, 0)
    column = jnp.broadcast_to(jnp.sum(mine.astype(F32), axis=1, keepdims=True), shape)
    va, vb = column.astype(I32), jnp.transpose(column).astype(I32)
    before = (sub % 16 < NEAR) & (va // LEAVES == vb // LEAVES) & (va < vb)
    slot = jnp.max(jnp.where(before, 1.0, 0.0), axis=0, keepdims=True).astype(I32)
    owner, place = vb[:1] // LEAVES, lane[:1] % 16
    shift = (z + 4 - owner // 4) % 4 * 4 + (y + 4 - owner % 4) % 4
    turn = jnp.zeros_like(shift)
    for at, k in enumerate(ORDER):
        turn = jnp.where(shift == k, at, turn)
    stage = jnp.where(turn < EARLY, 0, jnp.where(turn < MIDDLE, 1, 2))
    stage = jnp.where(place < NEAR, jnp.where(shift == 0, 3, stage), 4)
    key, code = stage * 16 + place, stage * STAGE + 2 * turn + slot
    same = sub // 16 == lane // 16
    rank = jnp.sum(jnp.where(same & (down(key) < key), 1.0, 0.0), axis=0, keepdims=True).astype(I32)
    chosen = jnp.where(same & (down(rank) == lane % 16), down(code), 0)
    return jnp.sum(chosen.astype(F32), axis=0, keepdims=True).astype(I32)


def progress(codes, l):
    first = both = remote = jnp.int32(0)
    for e in range(NEAR):
        code = codes[0, l * 16 + e]
        first += jnp.where(code < STAGE, 1, 0)
        both += jnp.where(code < 2 * STAGE, 1, 0)
        remote += jnp.where(code < 3 * STAGE, 1, 0)
    first = jnp.minimum(first, 4)
    return first, first + jnp.minimum(both - first, 4), remote


def listed_pairs(codes, l, start, width, limit, held, side, target):
    rows, weights = [], []
    spare = jnp.where(codes[0, l * 16 + start] < limit, codes[0, l * 16 + start], 0)
    for u in range(width):
        code = codes[0, l * 16 + start + u]
        real = code < limit
        slot = jnp.clip(jnp.where(real, code, spare) % STAGE, 0, held.shape[0] - 1)
        rows.append(jnp.concatenate((held[slot, :LEAF, :], side[slot]), axis=1))
        flag = jnp.where(real, 1.0, 0.0)
        weights.append((unpacked(held[slot, LEAF:, :]).astype(F32) * flag).astype(BF16))
    return weighted(jnp.concatenate(rows, axis=0), jnp.concatenate(weights, axis=1), target)


def exchange_kernel(
    points, charges, near, near_smem, interp_hbm, skel_leaf, mid_hbm, skel_mid, partners, top, skel_top,
    recv, total, targets, codes_out,
    interp, interp_mid, lists, list_in, charge_pack, send, own_side, skel_cols,
    mid_a, mid_b, scatter, scatter_in, gathered, crossed, early, held, side, codes,
    local_sem, list_s, list_r, near_s, near_r, ma_s, ma_r, mb_s, mb_r, sc_s, sc_r, ga_s, ga_r, cr_s, cr_r,
):
    me, group = lax.axis_index("sub"), lax.axis_index("leaf")
    z, y = me // 4, me % 4
    base = (group * N_SUB + me) * LEAVES

    def peer(k):
        return ((z + k // 4) % 4) * 4 + (y + k % 4) % 4

    def remote(src, dst, s, r, to):
        return pltpu.make_async_remote_copy(
            src_ref=src, dst_ref=dst, send_sem=s, recv_sem=r, device_id=to, device_id_type=MESH
        )

    def in_sub(src, dst, s, r, k):
        return remote(src, dst, s, r, (group, peer(k)))

    load_interp = pltpu.make_async_copy(interp_hbm, interp, local_sem.at[0])
    load_mid = pltpu.make_async_copy(mid_hbm, interp_mid, local_sem.at[1])
    load_interp.start()
    load_mid.start()

    barrier = pltpu.get_barrier_semaphore()
    for k in range(1, N_SUB):
        pl.semaphore_signal(barrier, inc=1, device_id=(group, peer(k)), device_id_type=MESH)
    for j in range(1, N_LEAF):
        pl.semaphore_signal(barrier, inc=1, device_id=((group + j) % N_LEAF, me), device_id_type=MESH)
    lists[...] = jnp.full(lists.shape, -1, I32)
    lists[:, :NEAR] = near[...]
    pl.semaphore_wait(barrier, N_SUB + N_LEAF - 2)

    list_copies = [None] + [
        in_sub(lists, list_in.at[k], list_s.at[k], list_r.at[k], k) for k in range(1, N_SUB)
    ]
    order = ORDER
    for k in order:
        list_copies[k].start()

    @pl.loop(0, LEAVES)
    def _(l):
        charge_pack[l] = packed(charges[:, pl.ds(pl.multiple_of(l * LEAF, LEAF), LEAF)])

    chosen = {}
    arrivals = {}

    def near_step(ks, s):
        started = []
        for k in ks:
            if s == 0:
                back = (-(k // 4)) % 4 * 4 + (-k) % 4
                list_copies[back].wait_recv()
                here = list_in[back] - base
                inside = (here >= 0) & (here < LEAVES)
                chosen[k] = (
                    jnp.min(jnp.where(inside, here, LEAVES - 1)),
                    jnp.max(jnp.where(inside, here, 0)),
                )
            leaf = chosen[k][s]
            send[k, s, :LEAF, :] = points[leaf]
            send[k, s, LEAF:, :] = charge_pack[leaf]
            at = 2 * ORDER.index(k) + s
            if at < 2 * EARLY:
                landing = early.at[at]
            elif at < 2 * MIDDLE:
                landing = held.at[at]
            else:
                landing = recv.at[at]
            c = in_sub(send.at[k, s], landing, near_s.at[k, s], near_r.at[k, s], k)
            c.start()
            started.append(c)
            arrivals[at] = c
        return started

    first, second = [], []

    def mid_step(ds):
        started = []
        for d in ds:
            started += [in_sub(mid_a.at[0], mid_a.at[d], ma_s.at[1, d], ma_r.at[1, d], 4 * d),
                        in_sub(mid_b.at[0], mid_b.at[d], mb_s.at[1, d], mb_r.at[1, d], d)]
        if not second:
            for c in first:
                c.wait_recv()
        for c in started:
            c.start()
        second.extend(started)
        return started

    steps = [(near_step, (ks, s)) for ks in GROUPS for s in range(2)]
    steps[10:10] = [(mid_step, ((1, 3),)), (mid_step, ((2,),))]
    taken = []

    def advance():
        t = len(taken)
        if t >= len(steps):
            return
        if t >= WINDOW:
            for c in taken[t - WINDOW]:
                c.wait_send()
        step, args = steps[t]
        taken.append(step(*args))

    for _ in range(WINDOW):
        advance()

    codes_out[...] = jnp.broadcast_to(sorted_lists(lists, group * N_SUB * LEAVES, z, y), codes_out.shape)
    save_codes = pltpu.make_async_copy(codes_out, codes, local_sem.at[2])
    save_codes.start()

    load_interp.wait()
    load_mid.wait()
    up = jnp.zeros((RHS, SKEL), F32)
    rows_in_leaf = lax.broadcasted_iota(I32, (LEAF, SKEL), 0)

    def upward(l, up):
        columns = jnp.transpose(points[l])
        targets[l] = target_side(columns)
        picks = jnp.where(rows_in_leaf == skel_leaf[pl.ds(l, 1), :], 1.0, 0.0).astype(BF16)
        skel_cols[l] = dot(columns, picks).astype(BF16)
        leaf_up = dot(unpacked(charge_pack[l]), interp[l]).astype(BF16)
        return up + dot(leaf_up, interp_mid[pl.ds(pl.multiple_of(l * SKEL, SKEL), SKEL), :])

    up = lax.fori_loop(0, LEAVES, upward, up)
    mid_up = up.astype(BF16)

    def pick_mid(l, cols):
        row = lax.broadcasted_iota(I32, (SKEL, SKEL), 0) + l * SKEL
        picks = jnp.where(row == skel_mid[...], 1.0, 0.0).astype(BF16)
        return cols + dot(skel_cols[l], picks)

    mid_cols = lax.fori_loop(0, LEAVES, pick_mid, jnp.zeros((DIM, SKEL), F32))
    mid_rows = jnp.transpose(mid_cols).astype(BF16)
    own_mid = jnp.concatenate((mid_rows, packed(mid_up)), axis=0)
    mid_a[0, 0] = own_mid[:HALF]
    mid_b[0, 0] = own_mid[HALF:]
    for d in (1, 3, 2):
        first.append(in_sub(mid_a.at[0, 0], mid_a.at[0, d], ma_s.at[0, d], ma_r.at[0, d], d))
        first.append(in_sub(mid_b.at[0, 0], mid_b.at[0, d], mb_s.at[0, d], mb_r.at[0, d], 4 * d))
    for c in first:
        c.start()

    row = lax.broadcasted_iota(I32, (SKEL, SKEL), 0) + me * SKEL
    picks = jnp.where(row == skel_top[...], 1.0, 0.0).astype(BF16)
    top_part = jnp.concatenate((dot(mid_up, top[...]), jnp.zeros((DIM - RHS, SKEL), F32)), axis=0)
    scatter[:, :DIM] = jnp.transpose(top_part)
    scatter[:, DIM:] = jnp.transpose(dot(mid_cols.astype(BF16), picks))
    piece = SKEL // N_SUB

    def rows_of(index):
        return pl.ds(pl.multiple_of(index * piece, piece), piece)

    scatter_copies = []
    for k in order:
        c = in_sub(scatter.at[rows_of(peer(k))], scatter_in.at[k], sc_s.at[k], sc_r.at[k], k)
        c.start()
        scatter_copies.append(c)
    advance()

    @pl.loop(0, LEAVES)
    def _(l):
        own_side[l] = source_side(points[l])

    def own_pairs(l):
        result = jnp.zeros((RHS, LEAF), F32)
        for part in range(0, LEAVES, 4):
            rows, weights = [], []
            for m in range(part, part + 4):
                named = near_smem[l, 0] == base + m
                for e in range(1, NEAR):
                    named = named | (near_smem[l, e] == base + m)
                flag = jnp.where(named, 1.0, 0.0)
                rows.append(jnp.concatenate((points[m], own_side[m]), axis=1))
                weights.append((unpacked(charge_pack[m]).astype(F32) * flag).astype(BF16))
            result += weighted(jnp.concatenate(rows, axis=0), jnp.concatenate(weights, axis=1), targets[l])
        total[l] = result

    def own_chunk(begin, end):
        pl.loop(begin, end)(own_pairs)

    own_chunk(0, 2)
    advance()
    own_chunk(2, 4)
    advance()

    for c in scatter_copies:
        c.wait_recv()
    summed = scatter[rows_of(me), :]
    for k in range(1, N_SUB):
        summed = summed + scatter_in[k]
    gathered[rows_of(me), :] = summed.astype(BF16)
    gather_copies = []
    for k in order:
        c = in_sub(gathered.at[rows_of(me)], gathered.at[rows_of(me)], ga_s.at[k], ga_r.at[k], k)
        c.start()
        gather_copies.append(c)

    advance()
    own_chunk(4, 6)
    advance()
    own_chunk(6, 8)
    advance()

    save_codes.wait()

    def arrived(begin, end):
        for at in range(2 * begin, 2 * end):
            arrivals[at].wait_recv()

    arrived(0, EARLY)
    keep_early = pltpu.make_async_copy(early, held.at[pl.ds(0, 2 * EARLY)], local_sem.at[3])
    keep_early.start()

    @pl.loop(0, 2 * EARLY)
    def _(i):
        side[i] = source_side(early[i, :LEAF, :])

    advance()

    def first_pass(l):
        total[l] += listed_pairs(codes, l, 0, 4, STAGE, early, side, targets[l])

    for begin in range(0, LEAVES, 2):
        pl.loop(begin, begin + 2)(first_pass)
        advance()
        if begin == 2:
            for c in gather_copies:
                c.wait_recv()
            cross_copies = []
            for j in (1, 7, 2, 6, 3, 5, 4):
                c = remote(gathered, crossed.at[j - 1], cr_s.at[j - 1], cr_r.at[j - 1], ((group + j) % N_LEAF, me))
                c.start()
                cross_copies.append(c)
    while len(taken) < len(steps):
        advance()

    for c in second:
        c.wait_recv()
    mid_targets = target_side(mid_cols.astype(BF16))
    rows, weights = [], []
    for p in range(4):
        node = partners[0, p] - group * N_SUB
        dz, dy = (z + 4 - node // 4) % 4, (y + 4 - node % 4) % 4
        block = jnp.concatenate((mid_a[dz, dy], mid_b[dy, dz]), axis=0)
        rows.append(jnp.concatenate((block[:SKEL], source_side(block[:SKEL])), axis=1))
        weights.append(unpacked(block[SKEL:]))
    mid_sum = weighted(jnp.concatenate(rows, axis=0), jnp.concatenate(weights, axis=1), mid_targets)

    for c in cross_copies:
        c.wait_recv()
    top_targets = target_side(jnp.transpose(gathered[:, DIM:].astype(F32)).astype(BF16))

    def top_from(j, acc):
        rows = crossed[j, :, DIM:]
        weights = jnp.transpose(crossed[j, :, :DIM].astype(F32)).astype(BF16)[:RHS]
        return acc + weighted(jnp.concatenate((rows, source_side(rows)), axis=1), weights, top_targets)

    top_sum = lax.fori_loop(0, N_LEAF - 1, top_from, jnp.zeros((RHS, SKEL), F32)).astype(BF16)
    mid_total = (mid_sum + dot_nt(top_sum, top[...])).astype(BF16)

    @pl.loop(0, LEAVES)
    def _(l):
        down = dot_nt(mid_total, interp_mid[pl.ds(pl.multiple_of(l * SKEL, SKEL), SKEL), :]).astype(BF16)
        total[l] += dot_nt(down, interp[l])

    keep_early.wait()

    def make_side(i):
        side[i] = source_side(held[i, :LEAF, :])

    for peers in ((EARLY, MIDDLE - 1), (MIDDLE - 1, MIDDLE)):
        arrived(*peers)
        pl.loop(2 * peers[0], 2 * peers[1])(make_side)
    keep_held = pltpu.make_async_copy(held, recv.at[pl.ds(0, 2 * MIDDLE)], local_sem.at[4])
    keep_held.start()

    @pl.loop(0, LEAVES)
    def _(l):
        start, _, _ = progress(codes, l)
        total[l] += listed_pairs(codes, l, start, 4, 2 * STAGE, held, side, targets[l])

    for copies in taken[len(steps) - WINDOW :]:
        for c in copies:
            c.wait_send()
    for c in list_copies[1:] + first + scatter_copies + gather_copies + cross_copies:
        c.wait_send()
    keep_held.wait()
    arrived(MIDDLE, N_SUB - 1)


def near_kernel(codes, recv, targets_hbm, total_hbm, out, held, side, used, targets, total, sem, load_sem):
    slots = held.shape[0]
    loads = (
        pltpu.make_async_copy(targets_hbm, targets, load_sem.at[0]),
        pltpu.make_async_copy(total_hbm, total, load_sem.at[1]),
    )
    for c in loads:
        c.start()
    for i in range(STAGE):
        used[i] = 0

    @pl.loop(0, LEAVES)
    def _(l):
        _, begin, end = progress(codes, l)
        for e in range(NEAR):
            slot = codes[0, l * 16 + e] % STAGE
            used[slot] = jnp.maximum(used[slot], jnp.where((begin <= e) & (e < end), 1, 0))

    def copy(i):
        return pltpu.make_async_copy(recv.at[i], held.at[i], sem.at[i])

    @pl.loop(0, slots)
    def _(i):
        pl.when(used[i] > 0)(lambda: copy(i).start())

    @pl.loop(0, slots)
    def _(i):
        @pl.when(used[i] > 0)
        def _():
            copy(i).wait()
            side[i] = source_side(held[i, :LEAF, :])

    for c in loads:
        c.wait()

    @pl.loop(0, LEAVES)
    def _(l):
        _, begin, end = progress(codes, l)

        def two(n, acc):
            return acc + listed_pairs(codes, l, begin + 2 * n, 2, 3 * STAGE, held, side, targets[l])

        acc = lax.fori_loop(0, (end - begin + 1) // 2, two, total[l])
        out[:, pl.ds(pl.multiple_of(l * LEAF, LEAF), LEAF)] = acc


def body(
    points, charges, near_leaves, leaf_interpolant, skel_leaf,
    interp_mid, skel_mid, mid_partners, interp_top, skel_top,
):
    vmem, smem, hbm = (pl.BlockSpec(memory_space=m) for m in (pltpu.VMEM, pltpu.SMEM, pl.ANY))
    dma = pltpu.SemaphoreType.DMA
    slots = 2 * (N_SUB - 1)
    recv, total, targets, codes = pl.pallas_call(
        exchange_kernel,
        out_shape=(
            jax.ShapeDtypeStruct((slots, SLOT, DIM), BF16),
            jax.ShapeDtypeStruct((LEAVES, RHS, LEAF), F32),
            jax.ShapeDtypeStruct((LEAVES, 2 * DIM, LEAF), BF16),
            jax.ShapeDtypeStruct((8, 128), I32),
        ),
        in_specs=[vmem, vmem, vmem, smem, hbm, vmem, hbm, vmem, smem, vmem, vmem],
        out_specs=(hbm, vmem, vmem, vmem),
        scratch_shapes=[
            pltpu.VMEM((LEAVES, LEAF, SKEL), BF16),
            pltpu.VMEM((LEAVES * SKEL, SKEL), BF16),
            pltpu.VMEM((LEAVES, DIM), I32),
            pltpu.VMEM((N_SUB, LEAVES, DIM), I32),
            pltpu.VMEM((LEAVES, PACKED, DIM), BF16),
            pltpu.VMEM((N_SUB, 2, SLOT, DIM), BF16),
            pltpu.VMEM((LEAVES, LEAF, DIM), BF16),
            pltpu.VMEM((LEAVES, DIM, SKEL), BF16),
            pltpu.VMEM((4, 4, HALF, DIM), BF16),
            pltpu.VMEM((4, 4, HALF, DIM), BF16),
            pltpu.VMEM((SKEL, 2 * DIM), F32),
            pltpu.VMEM((N_SUB, SKEL // N_SUB, 2 * DIM), F32),
            pltpu.VMEM((SKEL, 2 * DIM), BF16),
            pltpu.VMEM((N_LEAF - 1, SKEL, 2 * DIM), BF16),
            pltpu.VMEM((2 * EARLY, SLOT, DIM), BF16),
            pltpu.VMEM((2 * MIDDLE, SLOT, DIM), BF16),
            pltpu.VMEM((2 * MIDDLE, LEAF, DIM), BF16),
            pltpu.SMEM((8, 128), I32),
            dma((5,)),
            dma((N_SUB,)), dma((N_SUB,)),
            dma((N_SUB, 2)), dma((N_SUB, 2)),
            dma((2, 4)), dma((2, 4)), dma((2, 4)), dma((2, 4)),
            dma((N_SUB,)), dma((N_SUB,)),
            dma((N_SUB,)), dma((N_SUB,)),
            dma((N_LEAF - 1,)), dma((N_LEAF - 1,)),
        ],
        compiler_params=pltpu.CompilerParams(
            collective_id=0, has_side_effects=True, vmem_limit_bytes=56 << 20
        ),
    )(
        points.reshape(LEAVES, LEAF, DIM), charges.T, near_leaves, near_leaves,
        leaf_interpolant, skel_leaf, interp_mid[0], skel_mid, mid_partners, interp_top[0], skel_top,
    )
    out = pl.pallas_call(
        near_kernel,
        out_shape=jax.ShapeDtypeStruct((RHS, LEAVES * LEAF), F32),
        in_specs=[smem, hbm, hbm, hbm],
        out_specs=vmem,
        scratch_shapes=[
            pltpu.VMEM((slots, SLOT, DIM), BF16),
            pltpu.VMEM((slots, LEAF, DIM), BF16),
            pltpu.SMEM((STAGE,), I32),
            pltpu.VMEM((LEAVES, 2 * DIM, LEAF), BF16),
            pltpu.VMEM((LEAVES, RHS, LEAF), F32),
            dma((slots,)),
            dma((2,)),
        ],
        compiler_params=pltpu.CompilerParams(vmem_limit_bytes=56 << 20),
    )(codes, recv, targets, total)
    return out.T


def solution(mesh):
    placed = (
        P(("leaf", "sub"), None),
        P(("leaf", "sub"), None),
        P(("leaf", "sub"), None),
        P(("leaf", "sub"), None, None),
        P(("leaf", "sub"), None),
        P(("leaf", "sub"), None, None),
        P(("leaf", "sub"), None),
        P(("leaf", "sub"), None),
        P("leaf", "sub", None),
        P("leaf", None),
    )
    return jax.shard_map(
        body, mesh=mesh, in_specs=placed, out_specs=P(("leaf", "sub"), None), check_vma=False
    )
```
